256 devices in a mesh: row: 16 (over z, core), col: 16 (over x, y).
Axes of the slice: x: 4, y: 4, z: 8, core: 2. Of those that a mesh axis runs over, the one named last changes fastest.
Arguments:
- sire_index: int32 [2048], P('row'), may hold values from 0 to 8191
- dam_index: int32 [2048], P('row'), may hold values from -1 to 8191, as said below
- relatives: float32 [8192, 4, 2048], P('row', None, 'col'), may hold values from 0 to 1
- factor_blocks: float32 [6, 2048, 2048], P(None, 'row', 'col'), may hold values from -0.125 to 0.125
- inverses: float32 [4, 2048, 2048], P(None, 'col'), as said below
Outputs:
- relationship: float32 [4, 2048, 2048], P(None, 'col', 'row')
- border: float32 [4, 2048, 2048], P(None, 'col', 'row')
The draws below stay inside these ranges and needn't reach their ends.
Inputs may be any that keep to these rules, and one draw needn't show every extreme that they name: `dam_index`: -1 marks an unknown dam; every other value is a row of relatives. `inverses`: lower triangular, with diagonal entries of 0.6 to 1.4.
All inputs are finite; a program needn't handle non-finite values.
Results may differ from the reference program's by a relative error of at most 0.0001.
Values sent between devices are 32-bit elements; how exact they have to be, the bound alone decides.
No kernel may reach another device: no remote copies, remote signals or barrier semaphores. Data moves between devices by JAX's collectives and lax.ppermute only.
A program may use at most 64 MiB of HBM per device.

```python
import math
import jax
import jax.numpy as jnp
import numpy as np
from jax import lax

BLOCK = 2048
BLOCKS = 4
CALVES = 2048
ANIMALS = 8192
PAIRS = 6


def draw_dam_index(key, part):
    first, second = jax.random.split(jax.random.fold_in(key, 11))
    mothers = jax.random.randint(first, (CALVES,), 0, ANIMALS, dtype=jnp.int32)
    unknown = jax.random.randint(second, (CALVES,), 0, 8, dtype=jnp.int32)
    return jnp.where(unknown == 0, -1, mothers).astype(jnp.int32)


def draw_inverses(key, part):
    first, second = jax.random.split(jax.random.fold_in(key, 23))
    diagonal = jax.random.uniform(first, (BLOCKS, BLOCK), jnp.float32, 0.6, 1.4)
    spread = jax.random.normal(second, (BLOCKS, BLOCK, BLOCK), jnp.float32) * (0.6 / math.sqrt(BLOCK))
    rows_iota = lax.broadcasted_iota(jnp.int32, (BLOCK, BLOCK), 0)
    cols_iota = lax.broadcasted_iota(jnp.int32, (BLOCK, BLOCK), 1)
    lower = jnp.where(rows_iota > cols_iota, spread, 0.0)
    return lower + jnp.where(rows_iota == cols_iota, diagonal[:, :, None], 0.0)


def touch_ends(result, stream_key, smallest, largest):
    extent = result.shape
    place = [jax.random.randint(jax.random.fold_in(stream_key, axis), (), 0, extent[axis]) for axis in range(len(extent))]
    result = result.at[tuple(place)].set(smallest)
    longest = extent.index(max(extent))
    place[longest] = (place[longest] + 1) % extent[longest]
    return result.at[tuple(place)].set(largest)


def with_spikes(result, stream_key, source, target, parts, factor):
    owner, partner = [(jnp.arange(result.shape[position]) // (result.shape[position] // parts)).reshape([-1 if axis == position else 1 for axis in range(result.ndim)]) for position in (source, target)]
    chosen = jax.random.permutation(stream_key, parts)[partner]
    strong = (owner == chosen) | (owner == (partner + parts // 2) % parts)
    return jnp.where(strong, factor * result, result)


def level_of(own_key, shape, cuts, low, top_value):
    loudness, own = 1.0, jax.random.fold_in(own_key, 6)
    for dim, shards_of in cuts:
        steps = jnp.exp(jax.random.uniform(jax.random.fold_in(own, dim), (shards_of,), jnp.float32, low / len(cuts), top_value / len(cuts)))
        loudness = loudness * jnp.repeat(steps, shape[dim] // shards_of).reshape([-1 if axis == dim else 1 for axis in range(len(shape))])
    return loudness


def rank_table(count, lean):
    weights = [(1 << 20) // math.isqrt(standing ** lean) + 1 for standing in range(1, count + 1)]
    scale = 1 + sum(weights) // (1 << 30)
    return np.cumsum(np.array([max(1, weight // scale) for weight in weights]))


def skewed_ids(own_key, shape, count, skew):
    table = rank_table(count, skew)
    ticket = jax.random.randint(jax.random.fold_in(own_key, 1), shape, 0, int(table[count - 1]))
    standing = jnp.searchsorted(jnp.asarray(table, jnp.int32), ticket, side="right")
    return jax.random.permutation(jax.random.fold_in(own_key, 2), count)[standing].astype(jnp.int32)


def noise_with(key, dims, scale, limit, cuts, heavy, held_as=jnp.bfloat16):
    entries = scale * jax.random.normal(key, dims, jnp.float32)
    if cuts:
        entries = entries * level_of(key, dims, cuts, -0.22, 0.18)
    return jnp.clip(with_spikes(entries, jax.random.fold_in(key, 3), *heavy), -limit, limit).astype(held_as)


def setup_inputs(seed: int = 0) -> dict:
    splits = jax.random.split(jax.random.key(seed), 6)
    return {
        "sire_index": touch_ends(skewed_ids(splits[0], (CALVES,), ANIMALS, 2), jax.random.fold_in(splits[0], 3), 0, ANIMALS - 1).astype(jnp.int32),
        "dam_index": draw_dam_index(jax.random.fold_in(splits[5], 71), 0),
        "relatives": jnp.clip(1.0 * jax.random.uniform(splits[2], (ANIMALS, BLOCKS, BLOCK), jnp.float32) ** level_of(splits[2], (ANIMALS, BLOCKS, BLOCK), ((0, 16), (2, 16)), -0.2, 0.2), 0.0, 1.0),
        "factor_blocks": noise_with(splits[3], (PAIRS, BLOCK, BLOCK), (2 * BLOCK) ** -0.5, 0.125, ((1, 16), (2, 16)), (2, 1, 16, 2.0), jnp.float32),
        "inverses": draw_inverses(jax.random.fold_in(splits[5], 71), 0),
    }


def reference(sire_index, dam_index, relatives, factor_blocks, inverses):
    flat_rows = relatives.reshape(ANIMALS, BLOCKS * BLOCK)

    def parent_rows(index):
        clipped = jnp.maximum(index, 0).astype(jnp.int32)
        picked = jnp.take(flat_rows, clipped, axis=0)
        return jnp.where((index >= 0)[:, None], picked, jnp.zeros_like(picked))

    halves = 0.5 * parent_rows(sire_index) + 0.5 * parent_rows(dam_index)
    relationship = halves.T.reshape(BLOCKS, BLOCK, CALVES)
    solved = []
    for target in range(BLOCKS):
        remain = relationship[target]
        for source in range(target):
            remain = remain - jnp.dot(factor_blocks[target * (target - 1) // 2 + source], solved[source], precision=lax.Precision.HIGHEST, preferred_element_type=jnp.float32)
        solved.append(jnp.dot(inverses[target], remain, precision=lax.Precision.HIGHEST, preferred_element_type=jnp.float32))
    return relationship, jnp.stack(solved)
```

```python
import jax
import jax.numpy as jnp
from jax import lax
from jax.sharding import Mesh, PartitionSpec as P

ROW = ("z", "core")
COL = ("x", "y")
BLOCKS = 4


def product(left, right):
    return jnp.dot(left, right, precision=lax.Precision.HIGH, preferred_element_type=jnp.float32)


def pieces(value):
    high = lax.reduce_precision(value, 8, 7)
    rest = value - high
    middle = lax.reduce_precision(rest, 8, 7)
    return [part.astype(jnp.bfloat16) for part in (high, middle, rest - middle)]


def gather_col(block):
    copies = jnp.broadcast_to(block[None], (16,) + block.shape)
    return lax.all_to_all(copies, COL, 0, 0, tiled=True).reshape(-1, block.shape[1])


def scatter_sum_col(partial):
    parts = lax.all_to_all(partial, COL, 0, 0, tiled=True)
    return jnp.sum(parts.reshape(16, -1, partial.shape[1]), axis=0)


def per_device(sire_index, dam_index, relatives, factor_blocks, inverses):
    old_dev, blocks, width = relatives.shape
    calf_dev = sire_index.shape[0]
    core = lax.axis_index("core")
    me = lax.axis_index(ROW)

    whole = lax.all_gather(factor_blocks, ROW, axis=1, tiled=True)

    index = lax.all_gather(jnp.stack([sire_index, dam_index]), ROW, axis=0, tiled=False)
    ids = me * old_dev + lax.iota(jnp.int32, old_dev)
    sire = index[:, 0, :, None] == ids
    dam = index[:, 1, :, None] == ids
    picks = 0.5 * (sire.astype(jnp.float32) + dam.astype(jnp.float32))
    picks = picks.astype(jnp.bfloat16).reshape(-1, old_dev)

    def partial(first, count):
        rows = relatives[:, first : first + count, :].reshape(old_dev, count * width)
        total = 0.0
        for piece in pieces(rows):
            total = total + jnp.dot(picks, piece, preferred_element_type=jnp.float32)
        return total.reshape(8, 2, calf_dev, count * width)

    def over_core(terms):
        keep = lax.dynamic_index_in_dim(terms, core, 1, keepdims=False)
        give = lax.dynamic_index_in_dim(terms, 1 - core, 1, keepdims=False)
        return keep + lax.ppermute(give, "core", [(0, 1), (1, 0)])

    first = lax.all_to_all(over_core(partial(0, 1)), "z", 0, 0, tiled=False)
    relation = [jnp.sum(first, axis=0).T]
    later = over_core(partial(1, blocks - 1)).reshape(8 * calf_dev, -1)
    later = lax.psum_scatter(later, "z", scatter_dimension=0, tiled=True)
    for target in range(1, blocks):
        relation.append(later[:, (target - 1) * width : target * width].T)

    solved = []
    for target in range(blocks):
        remain = relation[target]
        if target > 0:
            terms = 0.0
            for source in range(target):
                block = whole[target * (target - 1) // 2 + source]
                terms = terms + product(block, solved[source])
            remain = remain - scatter_sum_col(terms)
        solved.append(product(inverses[target], gather_col(remain)))
    return jnp.stack(relation), jnp.stack(solved)


def solution(mesh):
    fine = Mesh(mesh.devices.reshape(8, 2, 4, 4), ROW + COL)
    return jax.shard_map(
        per_device,
        mesh=fine,
        in_specs=(
            P(ROW),
            P(ROW),
            P(ROW, None, COL),
            P(None, ROW, COL),
            P(None, COL, None),
        ),
        out_specs=(P(None, COL, ROW), P(None, COL, ROW)),
        check_vma=False,
    )
```

```python
import functools

import jax
import jax.numpy as jnp
from jax import lax
from jax.experimental import pallas as pl
from jax.experimental.pallas import tpu as pltpu
from jax.sharding import Mesh, PartitionSpec as P

ROW = ("z", "core")
COL = ("x", "y")
WIDE = 512
SIDE = 128
PART = 32
F32 = jnp.float32
BF16 = jnp.bfloat16
SMEM = pl.BlockSpec(memory_space=pltpu.SMEM)
VMEM = pl.BlockSpec(memory_space=pltpu.VMEM)


def pieces(value):
    high = lax.reduce_precision(value, 8, 7)
    rest = value - high
    middle = lax.reduce_precision(rest, 8, 7)
    return [part.astype(BF16) for part in (high, middle, rest - middle)]


def halves(value):
    high = value.astype(BF16)
    return high, (value - high.astype(F32)).astype(BF16)


def exchange(parts, axis):
    got = [parts[0], None, None, None]
    for step in (1, 2, 3):
        pairs = [(i, (i + step) % 4) for i in range(4)]
        got[4 - step] = lax.ppermute(parts[step], axis, pairs)
    return got


def select_kernel(count, here, index, rows, keep, give):
    core, base = here[2], here[3]
    ids = lax.broadcasted_iota(jnp.int32, (WIDE, SIDE), 0) + base

    def picks(owner):
        pair = index[owner]
        sire = jnp.where(ids == pair[0:1, :], 0.5, 0.0)
        dam = jnp.where(ids == pair[1:2, :], 0.5, 0.0)
        return (sire + dam).astype(BF16)

    @pl.loop(0, 8)
    def _(z):
        both = jnp.concatenate([picks(2 * z + core), picks(2 * z + 1 - core)], axis=1)
        size = count * SIDE
        total = jnp.dot(rows[:size], both, preferred_element_type=F32)
        for piece in (1, 2):
            total += jnp.dot(rows[piece * size : (piece + 1) * size], both, preferred_element_type=F32)
        for block in range(count):
            one = total[block * SIDE : (block + 1) * SIDE]
            keep[block, z] = one[:, :SIDE]
            give[block, z] = one[:, SIDE:]


def select(count, here, index, rows):
    shape = jax.ShapeDtypeStruct((count, 8, SIDE, SIDE), F32)
    return pl.pallas_call(
        functools.partial(select_kernel, count),
        out_shape=(shape, shape),
        in_specs=[SMEM, VMEM, VMEM],
        out_specs=(VMEM, VMEM),
        cost_estimate=pl.CostEstimate(
            flops=2 * 3 * count * SIDE * WIDE * 2048, bytes_accessed=count << 20, transcendentals=0
        ),
        compiler_params=pltpu.CompilerParams(vmem_limit_bytes=40 << 20),
        name="select",
    )(here, index, rows)


def step_kernel(plan, counts, here, *refs):
    rights, lefts, starts = counts
    right_refs = refs[: 4 * rights]
    left_refs = refs[4 * rights : 4 * rights + lefts]
    start_refs = refs[4 * rights + lefts : 4 * rights + lefts + starts]
    outs = refs[4 * rights + lefts + starts : 4 * rights + lefts + starts + 4]
    scratch = refs[4 * rights + lefts + starts + 4]
    x, y = here[0], here[1]
    layouts, groups, has_start = plan
    for right, layout in enumerate(layouts):
        for k in range(4):
            place = lax.rem(y + k, 4)
            high, low = halves(right_refs[4 * right + k][...])
            both = jnp.concatenate([high, low], axis=1)
            if layout == "whole":
                scratch[right, pl.ds(pl.multiple_of(place * SIDE, SIDE), SIDE)] = both
            else:
                for block in range(4):
                    spot = pl.multiple_of(block * SIDE + place * PART, PART)
                    scratch[right, pl.ds(spot, PART)] = both[block * PART : (block + 1) * PART]
    for s in range(4):
        spot = pl.multiple_of(lax.rem(x + s, 4) * SIDE, SIDE)
        for out, terms in enumerate(groups):
            total = None
            for right, kind, first in terms:
                if kind == "four":
                    left = left_refs[first + s][0]
                else:
                    left = left_refs[first][0, pl.ds(spot, SIDE)]
                high, low = halves(left)
                both = jnp.dot(high, scratch[right], preferred_element_type=F32)
                term = both[:, :SIDE] + both[:, SIDE:]
                term += jnp.dot(low, scratch[right, :, :SIDE], preferred_element_type=F32)
                total = term if total is None else total + term
            if has_start[out]:
                total += start_refs[s][out * SIDE : (out + 1) * SIDE]
            outs[s][out * SIDE : (out + 1) * SIDE] = total


def step(here, rights, groups, start=None, name="step"):
    args, specs, plan_groups = [], [], []
    for blocks, _ in rights:
        args += blocks
        specs += [pl.BlockSpec((SIDE, SIDE), lambda i: (0, 0))] * 4
    lefts = 0
    products = 0
    for terms in groups:
        plan_terms = []
        for right, (source, block) in terms:
            four = isinstance(source, list)
            plan_terms.append((right, "four" if four else "stack", lefts))
            for one in source if four else [source]:
                args.append(one)
                rows = SIDE if four else WIDE
                specs.append(pl.BlockSpec((1, rows, WIDE), lambda i, block=block: (block, 0, 0)))
                lefts += 1
            products += 1
        plan_groups.append(tuple(plan_terms))
    starts = 0
    if start is not None:
        starts = 4
        args += start
        specs += [pl.BlockSpec((start[0].shape[0], SIDE), lambda i: (0, 0))] * 4
    has_start = tuple(start is not None and out * SIDE < start[0].shape[0] for out in range(len(groups)))
    plan = (tuple(layout for _, layout in rights), tuple(plan_groups), has_start)
    shape = jax.ShapeDtypeStruct((len(groups) * SIDE, SIDE), F32)
    return pl.pallas_call(
        functools.partial(step_kernel, plan, (len(rights), lefts, starts)),
        out_shape=(shape,) * 4,
        grid=(1,),
        in_specs=[SMEM] + specs,
        out_specs=(pl.BlockSpec(shape.shape, lambda i: (0, 0)),) * 4,
        scratch_shapes=[pltpu.VMEM((len(rights), WIDE, 2 * SIDE), BF16)],
        cost_estimate=pl.CostEstimate(
            flops=2 * 4 * products * WIDE * WIDE * SIDE, bytes_accessed=products << 20, transcendentals=0
        ),
        compiler_params=pltpu.CompilerParams(vmem_limit_bytes=40 << 20),
        name=name,
    )(here, *args)


def per_device(sire_index, dam_index, relatives, factor_blocks, inverses):
    old_dev, blocks, _ = relatives.shape
    x, y, core = lax.axis_index("x"), lax.axis_index("y"), lax.axis_index("core")
    here = jnp.stack([x, y, core, lax.axis_index(ROW) * old_dev]).astype(jnp.int32)

    def ahead(position, s):
        return lax.rem(position + s, 4)

    sent = [lax.dynamic_slice_in_dim(factor_blocks, ahead(y, s) * PART, PART, 1) for s in range(4)]
    got = exchange(sent, "y")
    lanes = jnp.concatenate(got + got, axis=2)
    lanes = lax.dynamic_slice_in_dim(lanes, (4 - y) * SIDE, WIDE, 2)
    factor = lax.all_gather(lanes, ROW, axis=1, tiled=True)

    sent = [lax.dynamic_slice_in_dim(inverses, ahead(x, s) * WIDE, WIDE, 2) for s in range(4)]
    inverse = exchange(sent, "x")

    pair = jnp.stack([sire_index, dam_index])
    index = lax.all_to_all(jnp.broadcast_to(pair[None], (16, 2, SIDE)), ROW, 0, 0)

    def chosen(first, count):
        rows = relatives[:, first : first + count, :].reshape(old_dev, count * SIDE).T
        keep, give = select(count, here, index, jnp.concatenate(pieces(rows)))
        return keep + lax.ppermute(give, "core", [(0, 1), (1, 0)])

    relation0 = jnp.sum(lax.all_to_all(chosen(0, 1)[0], "z", 0, 0), axis=0)
    later = chosen(1, blocks - 1)
    relation = [relation0]
    for target in range(1, blocks):
        terms = later[target - 1].reshape(32, PART, SIDE)
        terms = lax.all_to_all(terms, ("z", "y"), 0, 0)
        relation.append(jnp.sum(terms.reshape(8, SIDE, SIDE), axis=0))

    def gather(block):
        return exchange([block] * 4, "y")

    def add_up(parts):
        return sum(exchange(parts, "x"))

    remain = relation0
    spread = {}
    solved = []
    for target in range(blocks):
        if target > 0:
            terms = []
            for source in range(target):
                terms.append((source, (factor, target * (target - 1) // 2 + source)))
            rights = [(spread[source], "whole") for source in range(target)]
            remain = relation[target] - add_up(step(here, rights, [terms]))
        layout = "whole" if target == 0 else "parts"
        own = add_up(step(here, [(gather(remain), layout)], [[(0, (inverse, target))]]))
        solved.append(own)
        if target + 1 < blocks:
            spread[target] = gather(own)

    split = jnp.stack(relation[1:]).reshape(blocks - 1, 4, PART, SIDE)
    sent = [lax.dynamic_index_in_dim(split, ahead(y, s), 1, keepdims=False) for s in range(4)]
    got = exchange(sent, "y")
    rows = jnp.stack(got + got, axis=1)
    rows = lax.dynamic_slice_in_dim(rows, 4 - y, 4, 1).reshape(blocks - 1, SIDE, SIDE)
    return jnp.concatenate([relation0[None], rows]), jnp.stack(solved)


def solution(mesh):
    fine = Mesh(mesh.devices.reshape(8, 2, 4, 4), ROW + COL)
    return jax.shard_map(
        per_device,
        mesh=fine,
        in_specs=(
            P(ROW),
            P(ROW),
            P(ROW, None, COL),
            P(None, ROW, COL),
            P(None, COL, None),
        ),
        out_specs=(P(None, COL, ROW), P(None, COL, ROW)),
        check_vma=False,
    )
```

```python
import functools

import jax
import jax.numpy as jnp
from jax import lax
from jax.experimental import pallas as pl
from jax.experimental.pallas import tpu as pltpu
from jax.sharding import Mesh, PartitionSpec as P

ROW = ("z", "core")
COL = ("x", "y")
WIDE = 512
SIDE = 128
PART = 32
HALF = 64
LIMIT = 24 << 20
F32 = jnp.float32
BF16 = jnp.bfloat16
SMEM = pl.BlockSpec(memory_space=pltpu.SMEM)
VMEM = pl.BlockSpec(memory_space=pltpu.VMEM)


def pieces(value):
    high = lax.reduce_precision(value, 8, 7)
    rest = value - high
    middle = lax.reduce_precision(rest, 8, 7)
    return [part.astype(BF16) for part in (high, middle, rest - middle)]


def halves(value):
    high = value.astype(BF16)
    return high, (value - high.astype(F32)).astype(BF16)


def exchange(parts, axis):
    got = [parts[0], None, None, None]
    for step in (1, 2, 3):
        pairs = [(i, (i + step) % 4) for i in range(4)]
        got[4 - step] = lax.ppermute(parts[step], axis, pairs)
    return got


def select_kernel(count, here, index, rows, after, keep, give):
    core, base = here[2], here[3]
    ids = lax.broadcasted_iota(jnp.int32, (WIDE, SIDE), 0) + base

    def picks(owner):
        pair = index[owner]
        sire = jnp.where(ids == pair[0:1, :], 0.5, 0.0)
        dam = jnp.where(ids == pair[1:2, :], 0.5, 0.0)
        return (sire + dam).astype(BF16)

    @pl.loop(0, 8)
    def _(z):
        both = jnp.concatenate([picks(2 * z + core), picks(2 * z + 1 - core)], axis=1)
        size = count * SIDE
        total = jnp.dot(rows[:size], both, preferred_element_type=F32)
        for piece in (1, 2):
            total += jnp.dot(rows[piece * size : (piece + 1) * size], both, preferred_element_type=F32)
        keep[z] = total[:, :SIDE]
        give[z] = total[:, SIDE:]


def select(count, here, index, rows, after):
    shape = jax.ShapeDtypeStruct((8, count * SIDE, SIDE), F32)
    return pl.pallas_call(
        functools.partial(select_kernel, count),
        out_shape=(shape, shape),
        in_specs=[SMEM, VMEM, VMEM, pl.BlockSpec(memory_space=pl.ANY)],
        out_specs=(VMEM, VMEM),
        cost_estimate=pl.CostEstimate(
            flops=2 * 3 * count * SIDE * WIDE * 2048, bytes_accessed=count << 20, transcendentals=0
        ),
        compiler_params=pltpu.CompilerParams(vmem_limit_bytes=LIMIT),
        name="select",
    )(here, index, rows, after)


def premultiply_kernel(pairs, here, *refs):
    factors, inverses = refs[:pairs], refs[pairs : 2 * pairs]
    outs, scratch = refs[2 * pairs + 1 : 2 * pairs + 5], refs[2 * pairs + 5]
    y = here[1]
    for pair in range(pairs):
        left, low = halves(factors[pair][0])
        right, right_low = halves(inverses[pair][0])
        total = jnp.dot(left, right, preferred_element_type=F32)
        total += jnp.dot(low, right, preferred_element_type=F32)
        total += jnp.dot(left, right_low, preferred_element_type=F32)
        scratch[...] = total
        for s in range(4):
            spot = pl.multiple_of(lax.rem(y + s, 4) * PART, PART)
            outs[s][pair] = scratch[pl.ds(spot, PART)]


def premultiply(here, factor_blocks, inverses, pairs, after):
    wide = inverses.shape[2]
    shape = jax.ShapeDtypeStruct((len(pairs), PART, wide), F32)
    return pl.pallas_call(
        functools.partial(premultiply_kernel, len(pairs)),
        out_shape=(shape,) * 4,
        grid=(1,),
        in_specs=[SMEM]
        + [pl.BlockSpec((1, SIDE, SIDE), lambda i, at=at: (at, 0, 0)) for at, _ in pairs]
        + [pl.BlockSpec((1, SIDE, wide), lambda i, at=at: (at, 0, 0)) for _, at in pairs]
        + [pl.BlockSpec(memory_space=pl.ANY)],
        out_specs=(pl.BlockSpec(shape.shape, lambda i: (0, 0, 0)),) * 4,
        scratch_shapes=[pltpu.VMEM((SIDE, wide), F32)],
        cost_estimate=pl.CostEstimate(
            flops=6 * len(pairs) * SIDE * SIDE * wide, bytes_accessed=len(pairs) << 21, transcendentals=0
        ),
        compiler_params=pltpu.CompilerParams(vmem_limit_bytes=LIMIT),
        name="premultiply",
    )(here, *[factor_blocks] * len(pairs), *[inverses] * len(pairs), after)


def combine_kernel(here, *refs):
    parts, outs, scratch = refs[:4], refs[5:9], refs[9]
    scratch[...] = parts[0][...] + parts[1][...] + parts[2][...] + parts[3][...]
    for s in range(4):
        spot = pl.multiple_of(lax.rem(here[0] + s, 4) * WIDE, WIDE)
        outs[s][...] = scratch[:, :, pl.ds(spot, WIDE)]


def combine(here, parts, after):
    count, rows, wide = parts[0].shape
    return pl.pallas_call(
        combine_kernel,
        out_shape=(jax.ShapeDtypeStruct((count, rows, WIDE), F32),) * 4,
        in_specs=[SMEM] + [VMEM] * 4 + [pl.BlockSpec(memory_space=pl.ANY)],
        out_specs=(VMEM,) * 4,
        scratch_shapes=[pltpu.VMEM((count, rows, wide), F32)],
        compiler_params=pltpu.CompilerParams(vmem_limit_bytes=LIMIT),
        name="combine",
    )(here, *parts, after)


def step_kernel(layouts, groups, counts, here, *refs):
    rights, lefts, stacks = counts
    right_refs = refs[: 4 * rights]
    left_refs = refs[4 * rights : 4 * rights + lefts]
    outs = refs[4 * rights + lefts : 4 * rights + lefts + 4]
    both, whole, joined, held, sems = refs[4 * rights + lefts + 4 :]
    x, y, core = here[0], here[1], here[2]

    copies = {}
    for terms in groups:
        for _, kind, first, block in terms:
            if kind == "stack":
                at = len(copies)
                copies[first] = at, pltpu.make_async_copy(left_refs[first].at[block], held.at[at], sems.at[at])
                copies[first][1].start()

    for right, layout in enumerate(layouts):
        if layout == "whole":
            for k in range(4):
                high, low = halves(right_refs[4 * right + k][...])
                spot = pl.multiple_of(lax.rem(y + k, 4) * SIDE, SIDE)
                both[right, pl.ds(spot, SIDE)] = jnp.concatenate([high, low], axis=1)
        else:
            for k in range(4):
                place = lax.rem(y + k, 4)
                for part in range(4):
                    spot = pl.multiple_of(part * SIDE + place * PART, PART)
                    joined[pl.ds(spot, PART)] = right_refs[4 * right + k][part * PART : (part + 1) * PART]
            for k in range(4):
                spot = pl.multiple_of(lax.rem(y + k, 4) * SIDE, SIDE)
                rest = right_refs[4 * right + k][SIDE : 2 * SIDE] - joined[pl.ds(spot, SIDE)]
                high, low = halves(rest)
                both[right, pl.ds(spot, SIDE)] = jnp.concatenate([high, low], axis=1)

    for out, terms in reversed(list(enumerate(groups))):
        total = None
        for right, kind, first, _ in terms:
            if kind == "inverse":
                left = jnp.concatenate([left_refs[first + i][0] for i in range(8)], axis=0)
            else:
                at, copy = copies[first]
                copy.wait()
                left = held[at]
            high, low = halves(left)
            wide = jnp.dot(high, both[right], preferred_element_type=F32)
            term = wide[:, :SIDE] + wide[:, SIDE:]
            term += jnp.dot(low, both[right, :, :SIDE], preferred_element_type=F32)
            total = term if total is None else total + term
        at = out * SIDE
        if terms[0][1] == "inverse":
            for s in range(4):
                for half, owner in enumerate((core, 1 - core)):
                    spot = pl.multiple_of(at + owner * HALF, HALF)
                    first = s * SIDE + half * HALF
                    outs[s][pl.ds(spot, HALF)] = total[first : first + HALF]
        else:
            whole[...] = total
            for s in range(4):
                spot = pl.multiple_of(lax.rem(x + s, 4) * SIDE, SIDE)
                outs[s][at : at + SIDE] = whole[pl.ds(spot, SIDE)]


def step(here, rights, groups):
    args, specs, plan = [], [], []
    for blocks, at, layout in rights:
        args += blocks
        rows = SIDE if layout == "whole" else 2 * SIDE
        specs += [pl.BlockSpec((rows, SIDE), lambda i, at=at: (at, 0))] * 4
    lefts = stacks = 0
    for terms in groups:
        kinds = []
        for right, source, block in terms:
            many = isinstance(source, list)
            kinds.append((right, "inverse" if many else "stack", lefts, block))
            if many:
                args += source
                specs += [pl.BlockSpec((1, HALF, WIDE), lambda i, block=block: (block, 0, 0))] * 8
                lefts += 8
            else:
                args.append(source)
                specs.append(pl.BlockSpec(memory_space=pltpu.HBM))
                lefts += 1
                stacks += 1
        plan.append(tuple(kinds))
    products = sum(len(terms) for terms in groups)
    shape = jax.ShapeDtypeStruct((len(groups) * SIDE, SIDE), F32)
    return pl.pallas_call(
        functools.partial(
            step_kernel, tuple(layout for _, _, layout in rights), tuple(plan), (len(rights), lefts, stacks)
        ),
        out_shape=(shape,) * 4,
        grid=(1,),
        in_specs=[SMEM] + specs,
        out_specs=(pl.BlockSpec(shape.shape, lambda i: (0, 0)),) * 4,
        scratch_shapes=[
            pltpu.VMEM((len(rights), WIDE, 2 * SIDE), BF16),
            pltpu.VMEM((WIDE, SIDE), F32),
            pltpu.VMEM((WIDE, SIDE), F32),
            pltpu.VMEM((max(stacks, 1), WIDE, WIDE), F32),
            pltpu.SemaphoreType.DMA((max(stacks, 1),)),
        ],
        cost_estimate=pl.CostEstimate(
            flops=6 * products * WIDE * WIDE * SIDE, bytes_accessed=products << 20, transcendentals=0
        ),
        compiler_params=pltpu.CompilerParams(vmem_limit_bytes=LIMIT),
        name="step",
    )(here, *args)


def per_device(sire_index, dam_index, relatives, factor_blocks, inverses):
    old_dev, blocks, _ = relatives.shape
    x, y, core = lax.axis_index("x"), lax.axis_index("y"), lax.axis_index("core")
    here = jnp.stack([x, y, core, lax.axis_index(ROW) * old_dev]).astype(jnp.int32)
    swap = [(0, 1), (1, 0)]

    def ahead(position, s):
        return lax.rem(position + s, 4)

    plain = [factor_blocks[at] for at in (0, 1, 3, 4)]
    plain = jnp.stack(plain)
    sent = [lax.dynamic_slice_in_dim(plain, ahead(y, s) * PART, PART, 1) for s in range(4)]
    got = exchange(sent, "y")
    lanes = jnp.concatenate(got + got, axis=2)
    lanes = lax.dynamic_slice_in_dim(lanes, (4 - y) * SIDE, WIDE, 2)
    factor = pltpu.with_memory_space_constraint(lax.all_gather(lanes, ROW, axis=1, tiled=True), pltpu.HBM)

    pair = jnp.stack([sire_index, dam_index])
    index = lax.all_to_all(jnp.broadcast_to(pair[None], (16, 2, SIDE)), ROW, 0, 0)

    def rows_of(first, count):
        rows = relatives[:, first : first + count, :].reshape(old_dev, count * SIDE).T
        return jnp.concatenate(pieces(rows))

    keep, give = select(1, here, index, rows_of(0, 1), lanes)
    first_terms = keep + lax.ppermute(give, "core", swap)
    relation0 = jnp.sum(lax.all_to_all(first_terms, "z", 0, 0), axis=0)

    keep, give = select(blocks - 1, here, index, rows_of(1, blocks - 1), first_terms)
    terms = keep + lax.ppermute(give, "core", swap)
    later = lax.psum_scatter(terms.reshape(-1, SIDE), "z", scatter_dimension=0, tiled=True)
    later = later.reshape(blocks - 1, SIDE, SIDE)

    sent = [lax.dynamic_slice(inverses, (0, core * HALF, ahead(x, s) * WIDE), (blocks, HALF, WIDE)) for s in range(4)]
    mine = exchange(sent, "x")
    other = [lax.dynamic_slice(inverses, (0, (1 - core) * HALF, x * WIDE), (blocks, HALF, WIDE))]
    other += [lax.ppermute(mine[k], "core", swap) for k in (1, 2, 3)]
    inverse = [one for k in range(4) for one in (mine[k], other[k])]

    def gather(*parts):
        return exchange([jnp.concatenate(parts)] * 4, "y")

    def add_up(parts):
        return sum(exchange(parts, "x"))

    right0 = gather(relation0)
    parts = step(here, [(right0, 0, "whole")], [[(0, inverse, 0)]])
    solved0 = add_up(parts)

    got = exchange(premultiply(here, factor_blocks, inverses, ((2, 1), (5, 2)), lanes), "y")
    sent = combine(here, got, parts[1])
    merged = lax.all_gather(sum(exchange(sent, "x")), ROW, axis=1, tiled=True)
    merged = pltpu.with_memory_space_constraint(merged, pltpu.HBM)

    right1 = gather(solved0)
    sums = add_up(step(here, [(right1, 0, "whole")], [[(0, factor, 0)]]))
    right2 = gather(sums, later[0])
    sums = add_up(
        step(
            here,
            [(right2, 0, "parts"), (right1, 0, "whole")],
            [[(0, merged, 0), (1, factor, 1)], [(0, inverse, 1)]],
        )
    )
    solved1 = sums[SIDE:]
    right3 = gather(sums[:SIDE], later[1], solved1)
    sums = add_up(
        step(
            here,
            [(right3, 0, "parts"), (right3, 2, "whole"), (right1, 0, "whole")],
            [[(0, merged, 1), (1, factor, 3), (2, factor, 2)], [(0, inverse, 2)]],
        )
    )
    solved2 = sums[SIDE:]
    right4 = gather(sums[:SIDE], later[2])
    solved3 = add_up(step(here, [(right4, 0, "parts")], [[(0, inverse, 3)]]))

    relationship = jnp.concatenate([relation0[None], later])
    return relationship, jnp.stack([solved0, solved1, solved2, solved3])


def solution(mesh):
    fine = Mesh(mesh.devices.reshape(8, 2, 4, 4), ROW + COL)
    return jax.shard_map(
        per_device,
        mesh=fine,
        in_specs=(
            P(ROW),
            P(ROW),
            P(ROW, None, COL),
            P(None, ROW, COL),
            P(None, COL, None),
        ),
        out_specs=(P(None, COL, ROW), P(None, COL, ROW)),
        check_vma=False,
    )
```

```python
import functools

import jax
import jax.numpy as jnp
from jax import lax
from jax.experimental import pallas as pl
from jax.experimental.pallas import tpu as pltpu
from jax.sharding import Mesh, PartitionSpec as P

ROW = ("z", "core")
COL = ("x", "y")
OLD = 512
SIDE = 128
GROUP = 16
LIMIT = 24 << 20
F32 = jnp.float32
BF16 = jnp.bfloat16
SMEM = pl.BlockSpec(memory_space=pltpu.SMEM)
VMEM = pl.BlockSpec(memory_space=pltpu.VMEM)
PARAMS = pltpu.CompilerParams(vmem_limit_bytes=LIMIT)


def pieces(value):
    high = lax.reduce_precision(value, 8, 7)
    rest = value - high
    middle = lax.reduce_precision(rest, 8, 7)
    return [part.astype(BF16) for part in (high, middle, rest - middle)]


def halves(value):
    high = value.astype(BF16)
    return high, (value - high.astype(F32)).astype(BF16)


def select_kernel(count, here, index, rows, after, keep, give):
    core, base = here[2], here[3]
    ids = lax.broadcasted_iota(jnp.int32, (OLD, SIDE), 0) + base

    def picks(owner):
        pair = index[owner]
        sire = jnp.where(ids == pair[0:1, :], 0.5, 0.0)
        dam = jnp.where(ids == pair[1:2, :], 0.5, 0.0)
        return (sire + dam).astype(BF16)

    @pl.loop(0, 8)
    def _(z):
        both = jnp.concatenate([picks(2 * z + core), picks(2 * z + 1 - core)], axis=1)
        size = count * SIDE
        total = jnp.dot(rows[:size], both, preferred_element_type=F32)
        for piece in (1, 2):
            total += jnp.dot(rows[piece * size : (piece + 1) * size], both, preferred_element_type=F32)
        keep[z] = total[:, :SIDE]
        give[z] = total[:, SIDE:]


def select(count, here, index, rows, after):
    shape = jax.ShapeDtypeStruct((8, count * SIDE, SIDE), F32)
    return pl.pallas_call(
        functools.partial(select_kernel, count),
        out_shape=(shape, shape),
        in_specs=[SMEM, VMEM, VMEM, pl.BlockSpec(memory_space=pl.ANY)],
        out_specs=(VMEM, VMEM),
        cost_estimate=pl.CostEstimate(
            flops=2 * 3 * count * SIDE * OLD * 2048, bytes_accessed=count << 20, transcendentals=0
        ),
        compiler_params=PARAMS,
        name="select",
    )(here, index, rows, after)


def remain_kernel(minus, *refs):
    terms = refs[0]
    total = terms[0]
    for part in range(1, terms.shape[0]):
        total += terms[part]
    if minus:
        total = refs[1][0] - total
    else:
        refs[1][...] = total
    for owner in range(GROUP):
        refs[2][owner] = total


def spread(terms, minuend=None, block=0):
    copies = jax.ShapeDtypeStruct((GROUP, SIDE, SIDE), F32)
    copies_spec = pl.BlockSpec(copies.shape, lambda i: (0, 0, 0))
    terms_spec = pl.BlockSpec(terms.shape, lambda i: (0, 0, 0))
    if minuend is None:
        return pl.pallas_call(
            functools.partial(remain_kernel, False),
            out_shape=(jax.ShapeDtypeStruct((SIDE, SIDE), F32), copies),
            grid=(1,),
            in_specs=[terms_spec],
            out_specs=(pl.BlockSpec((SIDE, SIDE), lambda i: (0, 0)), copies_spec),
            compiler_params=PARAMS,
            name="sum_first",
        )(terms)
    return pl.pallas_call(
        functools.partial(remain_kernel, True),
        out_shape=copies,
        grid=(1,),
        in_specs=[terms_spec, pl.BlockSpec((1, SIDE, SIDE), lambda i: (block, 0, 0))],
        out_specs=copies_spec,
        compiler_params=PARAMS,
        name="subtract",
    )(terms, minuend)


def solve_kernel(target, last, *refs):
    whole, inverse = refs[0], refs[1]
    factors = refs[2 : 2 + (0 if last else target + 1)]
    before = refs[2 + len(factors) : 2 + len(factors) + (0 if last else target)]
    solved = refs[2 + len(factors) + len(before)]
    high, low = halves(whole[...].reshape(GROUP * SIDE, SIDE))
    left, left_low = halves(inverse[0])
    wide = jnp.dot(left, jnp.concatenate([high, low], axis=1), preferred_element_type=F32)
    own = wide[:, :SIDE] + wide[:, SIDE:] + jnp.dot(left_low, high, preferred_element_type=F32)
    solved[...] = own
    if last:
        return
    terms = refs[-1]
    rights = [one[...] for one in before] + [own]
    for first in range(0, target + 1, 2):
        some = range(first, min(first + 2, target + 1))
        right = jnp.concatenate([rights[source] for source in some], axis=0)
        high, low = halves(right)
        right = jnp.concatenate([high, low], axis=1)
        for part in range(4):
            rows = pl.ds(part * 4 * SIDE, 4 * SIDE)
            left = jnp.concatenate([factors[source][0, rows] for source in some], axis=1)
            left, left_low = halves(left)
            wide = jnp.dot(left, right, preferred_element_type=F32)
            term = wide[:, :SIDE] + wide[:, SIDE:] + jnp.dot(left_low, high, preferred_element_type=F32)
            term = term.reshape(4, SIDE, SIDE)
            if first == 0:
                terms[pl.ds(part * 4, 4)] = term
            else:
                terms[pl.ds(part * 4, 4)] += term


def solve(target, whole, inverses, factor, before):
    last = target + 1 == inverses.shape[0]
    count = 0 if last else target + 1
    first = target * (target + 1) // 2
    one = jax.ShapeDtypeStruct((SIDE, SIDE), F32)
    one_spec = pl.BlockSpec(one.shape, lambda i: (0, 0))
    group = jax.ShapeDtypeStruct((GROUP, SIDE, SIDE), F32)
    group_spec = pl.BlockSpec(group.shape, lambda i: (0, 0, 0))
    out = pl.pallas_call(
        functools.partial(solve_kernel, target, last),
        out_shape=(one,) if last else (one, group),
        grid=(1,),
        in_specs=[group_spec, pl.BlockSpec((1, SIDE, GROUP * SIDE), lambda i: (target, 0, 0))]
        + [pl.BlockSpec((1, GROUP * SIDE, SIDE), lambda i, at=first + k: (at, 0, 0)) for k in range(count)]
        + [one_spec] * (0 if last else target),
        out_specs=(one_spec,) if last else (one_spec, group_spec),
        compiler_params=PARAMS,
        name="solve",
    )(whole, inverses, *[factor] * count, *([] if last else before))
    return (out[0], None) if last else out


def to_group(parts):
    return lax.all_to_all(parts, COL, 0, 0)


def per_device(sire_index, dam_index, relatives, factor_blocks, inverses):
    old_dev, blocks, _ = relatives.shape
    here = jnp.stack([jnp.int32(0), jnp.int32(0), lax.axis_index("core"), lax.axis_index(ROW) * old_dev])
    here = here.astype(jnp.int32)
    swap = [(0, 1), (1, 0)]

    factor = lax.all_gather(factor_blocks, ROW, axis=1, tiled=True)
    factor = pltpu.with_memory_space_constraint(factor, pltpu.HBM)
    inverses = pltpu.with_memory_space_constraint(inverses, pltpu.HBM)

    pair = jnp.stack([sire_index, dam_index])
    index = lax.all_to_all(jnp.broadcast_to(pair[None], (GROUP, 2, SIDE)), ROW, 0, 0)

    def rows_of(first, count):
        rows = relatives[:, first : first + count, :].reshape(old_dev, count * SIDE).T
        return jnp.concatenate(pieces(rows))

    keep, give = select(1, here, index, rows_of(0, 1), here)
    first_terms = keep + lax.ppermute(give, "core", swap)
    relation0, copies = spread(lax.all_to_all(first_terms, "z", 0, 0))

    keep, give = select(blocks - 1, here, index, rows_of(1, blocks - 1), first_terms)
    terms = keep + lax.ppermute(give, "core", swap)
    later = lax.psum_scatter(terms.reshape(-1, SIDE), "z", scatter_dimension=0, tiled=True)
    later = later.reshape(blocks - 1, SIDE, SIDE)

    solved = []
    for target in range(blocks):
        if target > 0:
            copies = spread(to_group(terms), later, target - 1)
        own, terms = solve(target, to_group(copies), inverses, factor, solved)
        solved.append(own)
    relationship = jnp.concatenate([relation0[None], later])
    return relationship, jnp.stack(solved)


def solution(mesh):
    fine = Mesh(mesh.devices.reshape(8, 2, 4, 4), ROW + COL)
    return jax.shard_map(
        per_device,
        mesh=fine,
        in_specs=(
            P(ROW),
            P(ROW),
            P(ROW, None, COL),
            P(None, ROW, COL),
            P(None, COL, None),
        ),
        out_specs=(P(None, COL, ROW), P(None, COL, ROW)),
        check_vma=False,
    )
```

```python
import functools

import jax
import jax.numpy as jnp
from jax import lax
from jax.experimental import pallas as pl
from jax.experimental.pallas import tpu as pltpu
from jax.sharding import Mesh, PartitionSpec as P

ROW = ("z", "core")
COL = ("x", "y")
OLD = 512
SIDE = 128
GROUP = 16
LIMIT = 24 << 20
F32 = jnp.float32
BF16 = jnp.bfloat16
SMEM = pl.BlockSpec(memory_space=pltpu.SMEM)
VMEM = pl.BlockSpec(memory_space=pltpu.VMEM)
PARAMS = pltpu.CompilerParams(vmem_limit_bytes=LIMIT)


def pieces(value):
    high = lax.reduce_precision(value, 8, 7)
    rest = value - high
    middle = lax.reduce_precision(rest, 8, 7)
    return [part.astype(BF16) for part in (high, middle, rest - middle)]


def halves(value):
    high = value.astype(BF16)
    return high, (value - high.astype(F32)).astype(BF16)


def select_kernel(count, here, index, rows, after, keep, give):
    core, base = here[2], here[3]
    ids = lax.broadcasted_iota(jnp.int32, (OLD, SIDE), 0) + base

    def picks(owner):
        pair = index[owner]
        sire = jnp.where(ids == pair[0:1, :], 0.5, 0.0)
        dam = jnp.where(ids == pair[1:2, :], 0.5, 0.0)
        return (sire + dam).astype(BF16)

    @pl.loop(0, 8)
    def _(z):
        both = jnp.concatenate([picks(2 * z + core), picks(2 * z + 1 - core)], axis=1)
        size = count * SIDE
        total = jnp.dot(rows[:size], both, preferred_element_type=F32)
        for piece in (1, 2):
            total += jnp.dot(rows[piece * size : (piece + 1) * size], both, preferred_element_type=F32)
        keep[z] = total[:, :SIDE]
        give[z] = total[:, SIDE:]


def select(count, here, index, rows, after):
    shape = jax.ShapeDtypeStruct((8, count * SIDE, SIDE), F32)
    return pl.pallas_call(
        functools.partial(select_kernel, count),
        out_shape=(shape, shape),
        in_specs=[SMEM, VMEM, VMEM, pl.BlockSpec(memory_space=pl.ANY)],
        out_specs=(VMEM, VMEM),
        cost_estimate=pl.CostEstimate(
            flops=2 * 3 * count * SIDE * OLD * 2048, bytes_accessed=count << 20, transcendentals=0
        ),
        compiler_params=PARAMS,
        name="select",
    )(here, index, rows, after)


def remain_kernel(block, *refs):
    terms = refs[0]
    total = terms[0]
    for part in range(1, terms.shape[0]):
        total += terms[part]
    if block is None:
        refs[1][...] = total
    else:
        total = refs[1][block] - total
    for owner in range(GROUP):
        refs[2][owner] = total


def spread(terms, minuend=None, block=None):
    copies = jax.ShapeDtypeStruct((GROUP, SIDE, SIDE), F32)
    if minuend is None:
        return pl.pallas_call(
            functools.partial(remain_kernel, None),
            out_shape=(jax.ShapeDtypeStruct((SIDE, SIDE), F32), copies),
            in_specs=[VMEM],
            out_specs=(VMEM, VMEM),
            compiler_params=PARAMS,
            name="sum_first",
        )(terms)
    return pl.pallas_call(
        functools.partial(remain_kernel, block),
        out_shape=copies,
        in_specs=[VMEM, VMEM],
        out_specs=VMEM,
        compiler_params=PARAMS,
        name="subtract",
    )(terms, minuend)


def solve_kernel(target, last, places, *refs):
    whole, inverse_ref = refs[0], refs[1]
    count = 0 if last else target + 1
    factors = refs[2 : 2 + count]
    before = refs[2 + count : 2 + count + target]
    solved = refs[2 + count + target]
    held_inverse, held, sems = refs[-3:]
    fetch = pltpu.make_async_copy(inverse_ref.at[target], held_inverse, sems.at[0])
    fetch.start()
    copies = []
    for source in range(count):
        copy = pltpu.make_async_copy(factors[source].at[places[source]], held.at[source], sems.at[source + 1])
        copy.start()
        copies.append(copy)

    high, low = halves(whole[...].reshape(GROUP * SIDE, SIDE))
    right = jnp.concatenate([high, low], axis=1)
    fetch.wait()
    left, left_low = halves(held_inverse[...])
    wide = jnp.dot(left, right, preferred_element_type=F32)
    own = wide[:, :SIDE] + wide[:, SIDE:] + jnp.dot(left_low, high, preferred_element_type=F32)
    if last:
        for source in range(target):
            solved[source] = before[source][...]
        solved[target] = own
        return
    solved[...] = own
    terms = refs[-4]
    rights = [one[...] for one in before] + [own]
    for first in range(0, count, 2):
        some = range(first, min(first + 2, count))
        right = jnp.concatenate([rights[source] for source in some], axis=0)
        high, low = halves(right)
        right = jnp.concatenate([high, low], axis=1)
        for source in some:
            copies[source].wait()
        for part in range(4):
            rows = pl.ds(part * 4 * SIDE, 4 * SIDE)
            left = jnp.concatenate([held[source, rows] for source in some], axis=1)
            left, left_low = halves(left)
            wide = jnp.dot(left, right, preferred_element_type=F32)
            term = wide[:, :SIDE] + wide[:, SIDE:] + jnp.dot(left_low, high, preferred_element_type=F32)
            term = term.reshape(4, SIDE, SIDE)
            if first == 0:
                terms[pl.ds(part * 4, 4)] = term
            else:
                terms[pl.ds(part * 4, 4)] += term


def solve(target, whole, inverses, factors, before):
    last = target + 1 == inverses.shape[0]
    count = len(factors)
    one = jax.ShapeDtypeStruct((SIDE, SIDE), F32)
    out_shape = (one, jax.ShapeDtypeStruct((GROUP, SIDE, SIDE), F32))
    if last:
        out_shape = (jax.ShapeDtypeStruct((target + 1, SIDE, SIDE), F32),)
    hbm = pl.BlockSpec(memory_space=pltpu.HBM)
    out = pl.pallas_call(
        functools.partial(solve_kernel, target, last, tuple(block for _, block in factors)),
        out_shape=out_shape,
        in_specs=[VMEM, hbm] + [hbm] * count + [VMEM] * target,
        out_specs=(VMEM,) * len(out_shape),
        scratch_shapes=[
            pltpu.VMEM((SIDE, GROUP * SIDE), F32),
            pltpu.VMEM((max(count, 1), GROUP * SIDE, SIDE), F32),
            pltpu.SemaphoreType.DMA((count + 1,)),
        ],
        compiler_params=PARAMS,
        name="solve",
    )(whole, inverses, *[array for array, _ in factors], *before)
    return (out[0], None) if last else out


def hold_kernel(blocks, after, out):
    out[...] = blocks[1:]


def hold(blocks, after):
    shape = jax.ShapeDtypeStruct((blocks.shape[0] - 1,) + blocks.shape[1:], F32)
    return pl.pallas_call(
        hold_kernel,
        out_shape=shape,
        in_specs=[VMEM, pl.BlockSpec(memory_space=pl.ANY)],
        out_specs=VMEM,
        compiler_params=PARAMS,
        name="hold",
    )(blocks, after)


def to_group(parts):
    return lax.all_to_all(parts, COL, 0, 0)


def per_device(sire_index, dam_index, relatives, factor_blocks, inverses):
    old_dev, blocks, _ = relatives.shape
    here = jnp.stack([jnp.int32(0), jnp.int32(0), lax.axis_index("core"), lax.axis_index(ROW) * old_dev])
    here = here.astype(jnp.int32)
    swap = [(0, 1), (1, 0)]

    def gathered(some):
        return pltpu.with_memory_space_constraint(lax.all_gather(some, ROW, axis=1, tiled=True), pltpu.HBM)

    start = gathered(factor_blocks[:1])
    inverses = pltpu.with_memory_space_constraint(inverses, pltpu.HBM)

    pair = jnp.stack([sire_index, dam_index])
    index = lax.all_to_all(jnp.broadcast_to(pair[None], (GROUP, 2, SIDE)), ROW, 0, 0)

    def rows_of(first, count):
        rows = relatives[:, first : first + count, :].reshape(old_dev, count * SIDE).T
        return jnp.concatenate(pieces(rows))

    keep, give = select(1, here, index, rows_of(0, 1), here)
    first_terms = keep + lax.ppermute(give, "core", swap)
    relation0, copies = spread(lax.all_to_all(first_terms, "z", 0, 0))

    rest = gathered(hold(factor_blocks, relation0))

    keep, give = select(blocks - 1, here, index, rows_of(1, blocks - 1), first_terms)
    terms = keep + lax.ppermute(give, "core", swap)
    later = lax.psum_scatter(terms.reshape(-1, SIDE), "z", scatter_dimension=0, tiled=True)
    later = later.reshape(blocks - 1, SIDE, SIDE)

    solved = []
    for target in range(blocks):
        if target > 0:
            copies = spread(to_group(terms), later, target - 1)
        first = target * (target + 1) // 2
        factors = [(rest, first + source - 1) for source in range(target + 1)]
        if target == 0:
            factors = [(start, 0)]
        if target + 1 == blocks:
            factors = []
        own, terms = solve(target, to_group(copies), inverses, factors, solved)
        solved.append(own)
    relationship = jnp.concatenate([relation0[None], later])
    return relationship, solved[-1]


def solution(mesh):
    fine = Mesh(mesh.devices.reshape(8, 2, 4, 4), ROW + COL)
    return jax.shard_map(
        per_device,
        mesh=fine,
        in_specs=(
            P(ROW),
            P(ROW),
            P(ROW, None, COL),
            P(None, ROW, COL),
            P(None, COL, None),
        ),
        out_specs=(P(None, COL, ROW), P(None, COL, ROW)),
        check_vma=False,
    )
```

```python
import functools

import jax
import jax.numpy as jnp
from jax import lax
from jax.experimental import pallas as pl
from jax.experimental.pallas import tpu as pltpu
from jax.sharding import Mesh, PartitionSpec as P

ROW = ("z", "core")
COL = ("x", "y")
OLD = 512
SIDE = 128
GROUP = 16
LIMIT = 24 << 20
F32 = jnp.float32
BF16 = jnp.bfloat16
SMEM = pl.BlockSpec(memory_space=pltpu.SMEM)
VMEM = pl.BlockSpec(memory_space=pltpu.VMEM)
PARAMS = pltpu.CompilerParams(vmem_limit_bytes=LIMIT)


def pieces(value):
    high = lax.reduce_precision(value, 8, 7)
    rest = value - high
    middle = lax.reduce_precision(rest, 8, 7)
    return [part.astype(BF16) for part in (high, middle, rest - middle)]


def halves(value):
    high = value.astype(BF16)
    return high, (value - high.astype(F32)).astype(BF16)


def select_kernel(count, here, index, rows, after, keep, give):
    core, base = here[2], here[3]
    ids = lax.broadcasted_iota(jnp.int32, (OLD, SIDE), 0) + base

    def picks(owner):
        pair = index[owner]
        sire = jnp.where(ids == pair[0:1, :], 0.5, 0.0)
        dam = jnp.where(ids == pair[1:2, :], 0.5, 0.0)
        return (sire + dam).astype(BF16)

    @pl.loop(0, 8)
    def _(z):
        both = jnp.concatenate([picks(2 * z + core), picks(2 * z + 1 - core)], axis=1)
        size = count * SIDE
        total = jnp.dot(rows[:size], both, preferred_element_type=F32)
        for piece in (1, 2):
            total += jnp.dot(rows[piece * size : (piece + 1) * size], both, preferred_element_type=F32)
        keep[z] = total[:, :SIDE]
        give[z] = total[:, SIDE:]


def select(count, here, index, rows, after):
    shape = jax.ShapeDtypeStruct((8, count * SIDE, SIDE), F32)
    return pl.pallas_call(
        functools.partial(select_kernel, count),
        out_shape=(shape, shape),
        in_specs=[SMEM, VMEM, VMEM, pl.BlockSpec(memory_space=pl.ANY)],
        out_specs=(VMEM, VMEM),
        cost_estimate=pl.CostEstimate(
            flops=2 * 3 * count * SIDE * OLD * 2048, bytes_accessed=count << 20, transcendentals=0
        ),
        compiler_params=PARAMS,
        name="select",
    )(here, index, rows, after)


def remain_kernel(block, *refs):
    terms = refs[0]
    total = terms[0]
    for part in range(1, terms.shape[0]):
        total += terms[part]
    if block is None:
        refs[1][...] = total
    else:
        total = refs[1][block] - total
    for owner in range(GROUP):
        refs[2][owner] = total


def spread(terms, minuend=None, block=None):
    copies = jax.ShapeDtypeStruct((GROUP, SIDE, SIDE), F32)
    if minuend is None:
        return pl.pallas_call(
            functools.partial(remain_kernel, None),
            out_shape=(jax.ShapeDtypeStruct((SIDE, SIDE), F32), copies),
            in_specs=[VMEM],
            out_specs=(VMEM, VMEM),
            compiler_params=PARAMS,
            name="sum_first",
        )(terms)
    return pl.pallas_call(
        functools.partial(remain_kernel, block),
        out_shape=copies,
        in_specs=[VMEM, VMEM],
        out_specs=VMEM,
        compiler_params=PARAMS,
        name="subtract",
    )(terms, minuend)


def solve_kernel(target, last, places, *refs):
    whole, inverse_ref = refs[0], refs[1]
    count = 0 if last else target + 1
    factors = refs[2 : 2 + count]
    before = refs[2 + count : 2 + count + target]
    solved = refs[2 + count + target]
    held_inverse, held, sems = refs[-3:]
    fetch = pltpu.make_async_copy(inverse_ref.at[target], held_inverse, sems.at[0])
    fetch.start()
    copies = []
    for source in range(count):
        copy = pltpu.make_async_copy(factors[source].at[places[source]], held.at[source], sems.at[source + 1])
        copy.start()
        copies.append(copy)

    high, low = halves(whole[...].reshape(GROUP * SIDE, SIDE))
    right = jnp.concatenate([high, low], axis=1)
    fetch.wait()
    left, left_low = halves(held_inverse[...])
    wide = jnp.dot(left, right, preferred_element_type=F32)
    own = wide[:, :SIDE] + wide[:, SIDE:] + jnp.dot(left_low, high, preferred_element_type=F32)
    if last:
        for source in range(target):
            solved[source] = before[source][...]
        solved[target] = own
        return
    solved[...] = own
    terms = refs[-4]
    rights = [one[...] for one in before] + [own]
    for first in range(0, count, 2):
        some = range(first, min(first + 2, count))
        right = jnp.concatenate([rights[source] for source in some], axis=0)
        high, low = halves(right)
        right = jnp.concatenate([high, low], axis=1)
        for source in some:
            copies[source].wait()
        for part in range(4):
            rows = pl.ds(part * 4 * SIDE, 4 * SIDE)
            left = jnp.concatenate([held[source, rows] for source in some], axis=1)
            left, left_low = halves(left)
            wide = jnp.dot(left, right, preferred_element_type=F32)
            term = wide[:, :SIDE] + wide[:, SIDE:] + jnp.dot(left_low, high, preferred_element_type=F32)
            term = term.reshape(4, SIDE, SIDE)
            if first == 0:
                terms[pl.ds(part * 4, 4)] = term
            else:
                terms[pl.ds(part * 4, 4)] += term


def solve(target, whole, inverses, factors, before):
    last = target + 1 == inverses.shape[0]
    count = len(factors)
    one = jax.ShapeDtypeStruct((SIDE, SIDE), F32)
    out_shape = (one, jax.ShapeDtypeStruct((GROUP, SIDE, SIDE), F32))
    if last:
        out_shape = (jax.ShapeDtypeStruct((target + 1, SIDE, SIDE), F32),)
    hbm = pl.BlockSpec(memory_space=pltpu.HBM)
    out = pl.pallas_call(
        functools.partial(solve_kernel, target, last, tuple(block for _, block in factors)),
        out_shape=out_shape,
        in_specs=[VMEM, hbm] + [hbm] * count + [VMEM] * target,
        out_specs=(VMEM,) * len(out_shape),
        scratch_shapes=[
            pltpu.VMEM((SIDE, GROUP * SIDE), F32),
            pltpu.VMEM((max(count, 1), GROUP * SIDE, SIDE), F32),
            pltpu.SemaphoreType.DMA((count + 1,)),
        ],
        compiler_params=PARAMS,
        name="solve",
    )(whole, inverses, *[array for array, _ in factors], *before)
    return (out[0], None) if last else out


def hold_kernel(blocks, after, out):
    out[...] = blocks[1:]


def hold(blocks, after):
    shape = jax.ShapeDtypeStruct((blocks.shape[0] - 1,) + blocks.shape[1:], F32)
    return pl.pallas_call(
        hold_kernel,
        out_shape=shape,
        in_specs=[VMEM, pl.BlockSpec(memory_space=pl.ANY)],
        out_specs=VMEM,
        compiler_params=PARAMS,
        name="hold",
    )(blocks, after)


def add_kernel(one, other, after, first, rest):
    first[...] = one[:, :SIDE] + other[:, :SIDE]
    rest[...] = one[:, SIDE:] + other[:, SIDE:]


def add(one, other, after):
    rest = (one.shape[0], one.shape[1] - SIDE, SIDE)
    return pl.pallas_call(
        add_kernel,
        out_shape=(jax.ShapeDtypeStruct((one.shape[0], SIDE, SIDE), F32), jax.ShapeDtypeStruct(rest, F32)),
        in_specs=[VMEM, VMEM, pl.BlockSpec(memory_space=pl.ANY)],
        out_specs=(VMEM, VMEM),
        compiler_params=PARAMS,
        name="add",
    )(one, other, after)


def pair_kernel(sire, dam, out):
    for owner in range(GROUP):
        out[owner, 0:1] = sire[...]
        out[owner, 1:2] = dam[...]


def to_group(parts):
    return lax.all_to_all(parts, COL, 0, 0)


def per_device(sire_index, dam_index, relatives, factor_blocks, inverses):
    old_dev, blocks, _ = relatives.shape
    here = jnp.stack([jnp.int32(0), jnp.int32(0), lax.axis_index("core"), lax.axis_index(ROW) * old_dev])
    here = here.astype(jnp.int32)
    swap = [(0, 1), (1, 0)]

    def gathered(some):
        return pltpu.with_memory_space_constraint(lax.all_gather(some, ROW, axis=1, tiled=True), pltpu.HBM)

    start = gathered(factor_blocks[:1])
    inverses = pltpu.with_memory_space_constraint(inverses, pltpu.HBM)

    pair = pl.pallas_call(
        pair_kernel,
        out_shape=jax.ShapeDtypeStruct((GROUP, 2, SIDE), jnp.int32),
        in_specs=[VMEM, VMEM],
        out_specs=VMEM,
        compiler_params=PARAMS,
        name="pair",
    )(sire_index[None], dam_index[None])
    index = lax.all_to_all(pair, ROW, 0, 0)

    def rows_of(first, count):
        rows = relatives[:, first : first + count, :].reshape(old_dev, count * SIDE).T
        return jnp.concatenate(pieces(rows))

    keep, give = select(1, here, index, rows_of(0, 1), here)
    first_terms = keep + lax.ppermute(give, "core", swap)
    relation0, copies = spread(lax.all_to_all(first_terms, "z", 0, 0))

    rest = gathered(hold(factor_blocks, relation0))

    keep, give = select(blocks - 1, here, index, rows_of(1, blocks - 1), first_terms)
    parts = add(keep, lax.ppermute(give, "core", swap), relation0)
    parts = [lax.psum_scatter(part.reshape(-1, SIDE), "z", scatter_dimension=0, tiled=True) for part in parts]
    later = [part.reshape(-1, SIDE, SIDE) for part in parts]
    minuends = [(later[0], 0), (later[1], 0), (later[1], 1)]

    solved = []
    for target in range(blocks):
        if target > 0:
            copies = spread(to_group(terms), *minuends[target - 1])
        first = target * (target + 1) // 2
        factors = [(rest, first + source - 1) for source in range(target + 1)]
        if target == 0:
            factors = [(start, 0)]
        if target + 1 == blocks:
            factors = []
        own, terms = solve(target, to_group(copies), inverses, factors, solved)
        solved.append(own)
    relationship = jnp.concatenate([relation0[None], *later])
    return relationship, solved[-1]


def solution(mesh):
    fine = Mesh(mesh.devices.reshape(8, 2, 4, 4), ROW + COL)
    return jax.shard_map(
        per_device,
        mesh=fine,
        in_specs=(
            P(ROW),
            P(ROW),
            P(ROW, None, COL),
            P(None, ROW, COL),
            P(None, COL, None),
        ),
        out_specs=(P(None, COL, ROW), P(None, COL, ROW)),
        check_vma=False,
    )
```

```python
import functools

import jax
import jax.numpy as jnp
from jax import lax
from jax.experimental import pallas as pl
from jax.experimental.pallas import tpu as pltpu
from jax.sharding import Mesh, PartitionSpec as P

ROW = ("z", "core")
COL = ("x", "y")
OLD = 512
SIDE = 128
GROUP = 16
LIMIT = 24 << 20
F32 = jnp.float32
BF16 = jnp.bfloat16
SMEM = pl.BlockSpec(memory_space=pltpu.SMEM)
VMEM = pl.BlockSpec(memory_space=pltpu.VMEM)
HBM = pl.BlockSpec(memory_space=pltpu.HBM)
PARAMS = pltpu.CompilerParams(vmem_limit_bytes=LIMIT)


def pieces(value):
    high = lax.reduce_precision(value, 8, 7)
    rest = value - high
    middle = lax.reduce_precision(rest, 8, 7)
    return [part.astype(BF16) for part in (high, middle, rest - middle)]


def halves(value):
    high = value.astype(BF16)
    return high, (value - high.astype(F32)).astype(BF16)


def select_kernel(count, here, index, rows, after, keep, give):
    core, base = here[2], here[3]
    ids = lax.broadcasted_iota(jnp.int32, (OLD, SIDE), 0) + base

    def picks(owner):
        pair = index[owner]
        sire = jnp.where(ids == pair[0:1, :], 0.5, 0.0)
        dam = jnp.where(ids == pair[1:2, :], 0.5, 0.0)
        return (sire + dam).astype(BF16)

    @pl.loop(0, 8)
    def _(z):
        both = jnp.concatenate([picks(2 * z + core), picks(2 * z + 1 - core)], axis=1)
        size = count * SIDE
        total = jnp.dot(rows[:size], both, preferred_element_type=F32)
        for piece in (1, 2):
            total += jnp.dot(rows[piece * size : (piece + 1) * size], both, preferred_element_type=F32)
        keep[z] = total[:, :SIDE]
        give[z] = total[:, SIDE:]


def select(count, here, index, rows, after):
    shape = jax.ShapeDtypeStruct((8, count * SIDE, SIDE), F32)
    return pl.pallas_call(
        functools.partial(select_kernel, count),
        out_shape=(shape, shape),
        in_specs=[SMEM, VMEM, VMEM, pl.BlockSpec(memory_space=pl.ANY)],
        out_specs=(VMEM, VMEM),
        cost_estimate=pl.CostEstimate(
            flops=2 * 3 * count * SIDE * OLD * 2048, bytes_accessed=count << 20, transcendentals=0
        ),
        compiler_params=PARAMS,
        name="select",
    )(here, index, rows, after)


def in_hbm(array):
    return pltpu.with_memory_space_constraint(array, pltpu.HBM)


def added(terms):
    total = terms[0]
    for part in range(1, terms.shape[0]):
        total += terms[part]
    return total


def first_kernel(terms, total_ref, copies):
    total = added(terms)
    total_ref[...] = total
    for owner in range(GROUP):
        copies[owner] = total


def spread_first(terms):
    return pl.pallas_call(
        first_kernel,
        out_shape=(
            jax.ShapeDtypeStruct((SIDE, SIDE), F32),
            jax.ShapeDtypeStruct((GROUP, SIDE, SIDE), F32),
        ),
        in_specs=[VMEM],
        out_specs=(VMEM, VMEM),
        compiler_params=PARAMS,
        name="sum_first",
    )(terms)


def subtract_kernel(block, terms, minuend, copies, held, sem):
    fetch = pltpu.make_async_copy(minuend.at[block], held, sem.at[0])
    fetch.start()
    total = added(terms)
    fetch.wait()
    total = held[...] - total
    for owner in range(GROUP):
        copies[owner] = total


def spread(terms, minuend, block):
    return pl.pallas_call(
        functools.partial(subtract_kernel, block),
        out_shape=jax.ShapeDtypeStruct((GROUP, SIDE, SIDE), F32),
        in_specs=[VMEM, HBM],
        out_specs=VMEM,
        scratch_shapes=[pltpu.VMEM((SIDE, SIDE), F32), pltpu.SemaphoreType.DMA((1,))],
        compiler_params=PARAMS,
        name="subtract",
    )(terms, in_hbm(minuend))


def first_block_kernel(blocks, out, sem):
    copy = pltpu.make_async_copy(blocks.at[0:1], out, sem.at[0])
    copy.start()
    copy.wait()


def first_block(blocks):
    return pl.pallas_call(
        first_block_kernel,
        out_shape=jax.ShapeDtypeStruct((1,) + blocks.shape[1:], F32),
        in_specs=[HBM],
        out_specs=HBM,
        scratch_shapes=[pltpu.SemaphoreType.DMA((1,))],
        compiler_params=PARAMS,
        name="first_block",
    )(in_hbm(blocks))


def pair_kernel(sire, dam, after, pair, held, sems):
    copies = [
        pltpu.make_async_copy(sire, held.at[0:1], sems.at[0]),
        pltpu.make_async_copy(dam, held.at[1:2], sems.at[1]),
    ]
    for copy in copies:
        copy.start()
    for copy in copies:
        copy.wait()
    for owner in range(GROUP):
        pair[owner] = held[...]


def pair_copies(sire, dam, after):
    return pl.pallas_call(
        pair_kernel,
        out_shape=jax.ShapeDtypeStruct((GROUP, 2, SIDE), jnp.int32),
        in_specs=[HBM, HBM, pl.BlockSpec(memory_space=pl.ANY)],
        out_specs=VMEM,
        scratch_shapes=[pltpu.VMEM((2, SIDE), jnp.int32), pltpu.SemaphoreType.DMA((2,))],
        compiler_params=PARAMS,
        name="pair",
    )(in_hbm(sire), in_hbm(dam), after)


def add_kernel(one, other, after, out):
    out[...] = one[...] + other[...]


def add(one, other, after):
    return pl.pallas_call(
        add_kernel,
        out_shape=jax.ShapeDtypeStruct(one.shape, F32),
        in_specs=[VMEM, VMEM, pl.BlockSpec(memory_space=pl.ANY)],
        out_specs=VMEM,
        compiler_params=PARAMS,
        name="add",
    )(one, other, after)


def solve_kernel(target, last, places, *refs):
    whole, inverse_ref = refs[0], refs[1]
    count = 0 if last else target + 1
    factors = refs[2 : 2 + count]
    before = refs[2 + count : 2 + count + target]
    solved = refs[2 + count + target]
    held_inverse, held, sems = refs[-3:]
    fetch = pltpu.make_async_copy(inverse_ref.at[target], held_inverse, sems.at[0])
    fetch.start()
    copies = []
    for source in range(count):
        copy = pltpu.make_async_copy(factors[source].at[places[source]], held.at[source], sems.at[source + 1])
        copy.start()
        copies.append(copy)

    high, low = halves(whole[...].reshape(GROUP * SIDE, SIDE))
    right = jnp.concatenate([high, low], axis=1)
    fetch.wait()
    left, left_low = halves(held_inverse[...])
    wide = jnp.dot(left, right, preferred_element_type=F32)
    own = wide[:, :SIDE] + wide[:, SIDE:] + jnp.dot(left_low, high, preferred_element_type=F32)
    if last:
        for source in range(target):
            solved[source] = before[source][...]
        solved[target] = own
        return
    solved[...] = own
    terms = refs[-4]
    rights = [one[...] for one in before] + [own]
    for first in range(0, count, 2):
        some = range(first, min(first + 2, count))
        right = jnp.concatenate([rights[source] for source in some], axis=0)
        high, low = halves(right)
        right = jnp.concatenate([high, low], axis=1)
        for source in some:
            copies[source].wait()
        for part in range(4):
            rows = pl.ds(part * 4 * SIDE, 4 * SIDE)
            left = jnp.concatenate([held[source, rows] for source in some], axis=1)
            left, left_low = halves(left)
            wide = jnp.dot(left, right, preferred_element_type=F32)
            term = wide[:, :SIDE] + wide[:, SIDE:] + jnp.dot(left_low, high, preferred_element_type=F32)
            term = term.reshape(4, SIDE, SIDE)
            if first == 0:
                terms[pl.ds(part * 4, 4)] = term
            else:
                terms[pl.ds(part * 4, 4)] += term


def solve(target, whole, inverses, factors, before):
    last = target + 1 == inverses.shape[0]
    count = len(factors)
    one = jax.ShapeDtypeStruct((SIDE, SIDE), F32)
    out_shape = (one, jax.ShapeDtypeStruct((GROUP, SIDE, SIDE), F32))
    if last:
        out_shape = (jax.ShapeDtypeStruct((target + 1, SIDE, SIDE), F32),)
    hbm = pl.BlockSpec(memory_space=pltpu.HBM)
    out = pl.pallas_call(
        functools.partial(solve_kernel, target, last, tuple(block for _, block in factors)),
        out_shape=out_shape,
        in_specs=[VMEM, hbm] + [hbm] * count + [VMEM] * target,
        out_specs=(VMEM,) * len(out_shape),
        scratch_shapes=[
            pltpu.VMEM((SIDE, GROUP * SIDE), F32),
            pltpu.VMEM((max(count, 1), GROUP * SIDE, SIDE), F32),
            pltpu.SemaphoreType.DMA((count + 1,)),
        ],
        compiler_params=PARAMS,
        name="solve",
    )(whole, inverses, *[array for array, _ in factors], *before)
    return (out[0], None) if last else out


def hold_kernel(blocks, after, out):
    out[...] = blocks[1:]


def hold(blocks, after):
    shape = jax.ShapeDtypeStruct((blocks.shape[0] - 1,) + blocks.shape[1:], F32)
    return pl.pallas_call(
        hold_kernel,
        out_shape=shape,
        in_specs=[VMEM, pl.BlockSpec(memory_space=pl.ANY)],
        out_specs=VMEM,
        compiler_params=PARAMS,
        name="hold",
    )(blocks, after)


def to_group(parts):
    return lax.all_to_all(parts, COL, 0, 0)


def per_device(sire_index, dam_index, relatives, factor_blocks, inverses):
    old_dev, blocks, _ = relatives.shape
    here = jnp.stack([jnp.int32(0), jnp.int32(0), lax.axis_index("core"), lax.axis_index(ROW) * old_dev])
    here = here.astype(jnp.int32)
    swap = [(0, 1), (1, 0)]

    def gathered(some):
        return pltpu.with_memory_space_constraint(lax.all_gather(some, ROW, axis=1, tiled=True), pltpu.HBM)

    inverses = pltpu.with_memory_space_constraint(inverses, pltpu.HBM)
    first = first_block(factor_blocks)
    start = gathered(first)
    index = lax.all_to_all(pair_copies(sire_index[None], dam_index[None], first), ROW, 0, 0)

    def rows_of(first, count):
        rows = relatives[:, first : first + count, :].reshape(old_dev, count * SIDE).T
        return jnp.concatenate(pieces(rows))

    keep, give = select(1, here, index, rows_of(0, 1), here)
    first_terms = keep + lax.ppermute(give, "core", swap)
    relation0, copies = spread_first(lax.all_to_all(first_terms, "z", 0, 0))

    whole = to_group(copies)
    rest = gathered(hold(factor_blocks, whole))

    keep, give = select(blocks - 1, here, index, rows_of(1, blocks - 1), first_terms)
    terms = add(keep, lax.ppermute(give, "core", swap), relation0)
    later = lax.psum_scatter(terms.reshape(-1, SIDE), "z", scatter_dimension=0, tiled=True)
    later = later.reshape(blocks - 1, SIDE, SIDE)

    solved = []
    for target in range(blocks):
        if target > 0:
            whole = to_group(spread(to_group(terms), later, target - 1))
        first = target * (target + 1) // 2
        factors = [(rest, first + source - 1) for source in range(target + 1)]
        if target == 0:
            factors = [(start, 0)]
        if target + 1 == blocks:
            factors = []
        own, terms = solve(target, whole, inverses, factors, solved)
        solved.append(own)
    relationship = jnp.concatenate([relation0[None], later])
    return relationship, solved[-1]


def solution(mesh):
    fine = Mesh(mesh.devices.reshape(8, 2, 4, 4), ROW + COL)
    return jax.shard_map(
        per_device,
        mesh=fine,
        in_specs=(
            P(ROW),
            P(ROW),
            P(ROW, None, COL),
            P(None, ROW, COL),
            P(None, COL, None),
        ),
        out_specs=(P(None, COL, ROW), P(None, COL, ROW)),
        check_vma=False,
    )
```

```python
import functools

import jax
import jax.numpy as jnp
from jax import lax
from jax.experimental import pallas as pl
from jax.experimental.pallas import tpu as pltpu
from jax.sharding import Mesh, PartitionSpec as P

ROW = ("z", "core")
COL = ("x", "y")
OLD = 512
SIDE = 128
GROUP = 16
LIMIT = 24 << 20
F32 = jnp.float32
BF16 = jnp.bfloat16
SMEM = pl.BlockSpec(memory_space=pltpu.SMEM)
VMEM = pl.BlockSpec(memory_space=pltpu.VMEM)
HBM = pl.BlockSpec(memory_space=pltpu.HBM)
PARAMS = pltpu.CompilerParams(vmem_limit_bytes=LIMIT)


def pieces(value):
    high = lax.reduce_precision(value, 8, 7)
    rest = value - high
    middle = lax.reduce_precision(rest, 8, 7)
    return [part.astype(BF16) for part in (high, middle, rest - middle)]


def halves(value):
    high = value.astype(BF16)
    return high, (value - high.astype(F32)).astype(BF16)


def select_kernel(count, here, index, rows, after, keep, give):
    core, base = here[2], here[3]
    ids = lax.broadcasted_iota(jnp.int32, (OLD, SIDE), 0) + base

    def picks(owner):
        pair = index[owner]
        sire = jnp.where(ids == pair[0:1, :], 0.5, 0.0)
        dam = jnp.where(ids == pair[1:2, :], 0.5, 0.0)
        return (sire + dam).astype(BF16)

    @pl.loop(0, 8)
    def _(z):
        both = jnp.concatenate([picks(2 * z + core), picks(2 * z + 1 - core)], axis=1)
        size = count * SIDE
        total = jnp.dot(rows[:size], both, preferred_element_type=F32)
        for piece in (1, 2):
            total += jnp.dot(rows[piece * size : (piece + 1) * size], both, preferred_element_type=F32)
        keep[z] = total[:, :SIDE]
        give[z] = total[:, SIDE:]


def select(count, here, index, rows, after):
    shape = jax.ShapeDtypeStruct((8, count * SIDE, SIDE), F32)
    return pl.pallas_call(
        functools.partial(select_kernel, count),
        out_shape=(shape, shape),
        in_specs=[SMEM, VMEM, VMEM, pl.BlockSpec(memory_space=pl.ANY)],
        out_specs=(VMEM, VMEM),
        cost_estimate=pl.CostEstimate(
            flops=2 * 3 * count * SIDE * OLD * 2048, bytes_accessed=count << 20, transcendentals=0
        ),
        compiler_params=PARAMS,
        name="select",
    )(here, index, rows, after)


def in_hbm(array):
    return pltpu.with_memory_space_constraint(array, pltpu.HBM)


def added(terms):
    total = terms[0]
    for part in range(1, terms.shape[0]):
        total += terms[part]
    return total


def first_kernel(terms, total_ref, copies):
    total = added(terms)
    total_ref[...] = total
    for owner in range(GROUP):
        copies[owner] = total


def spread_first(terms):
    return pl.pallas_call(
        first_kernel,
        out_shape=(
            jax.ShapeDtypeStruct((SIDE, SIDE), F32),
            jax.ShapeDtypeStruct((GROUP, SIDE, SIDE), F32),
        ),
        in_specs=[VMEM],
        out_specs=(VMEM, VMEM),
        compiler_params=PARAMS,
        name="sum_first",
    )(terms)


def subtract_kernel(block, terms, minuend, copies, held, sem):
    fetch = pltpu.make_async_copy(minuend.at[block], held, sem.at[0])
    fetch.start()
    total = added(terms)
    fetch.wait()
    total = held[...] - total
    for owner in range(GROUP):
        copies[owner] = total


def spread(terms, minuend, block):
    return pl.pallas_call(
        functools.partial(subtract_kernel, block),
        out_shape=jax.ShapeDtypeStruct((GROUP, SIDE, SIDE), F32),
        in_specs=[VMEM, HBM],
        out_specs=VMEM,
        scratch_shapes=[pltpu.VMEM((SIDE, SIDE), F32), pltpu.SemaphoreType.DMA((1,))],
        compiler_params=PARAMS,
        name="subtract",
    )(terms, in_hbm(minuend))


def first_block_kernel(blocks, out, sem):
    copy = pltpu.make_async_copy(blocks.at[0:1], out, sem.at[0])
    copy.start()
    copy.wait()


def first_block(blocks):
    return pl.pallas_call(
        first_block_kernel,
        out_shape=jax.ShapeDtypeStruct((1,) + blocks.shape[1:], F32),
        in_specs=[HBM],
        out_specs=VMEM,
        scratch_shapes=[pltpu.SemaphoreType.DMA((1,))],
        compiler_params=PARAMS,
        name="first_block",
    )(in_hbm(blocks))


def pair_kernel(sire, dam, after, pair, held, sems):
    copies = [
        pltpu.make_async_copy(sire, held.at[0:1], sems.at[0]),
        pltpu.make_async_copy(dam, held.at[1:2], sems.at[1]),
    ]
    for copy in copies:
        copy.start()
    for copy in copies:
        copy.wait()
    for owner in range(GROUP):
        pair[owner] = held[...]


def pair_copies(sire, dam, after):
    return pl.pallas_call(
        pair_kernel,
        out_shape=jax.ShapeDtypeStruct((GROUP, 2, SIDE), jnp.int32),
        in_specs=[HBM, HBM, pl.BlockSpec(memory_space=pl.ANY)],
        out_specs=VMEM,
        scratch_shapes=[pltpu.VMEM((2, SIDE), jnp.int32), pltpu.SemaphoreType.DMA((2,))],
        compiler_params=PARAMS,
        name="pair",
    )(in_hbm(sire), in_hbm(dam), after)


def add_kernel(one, other, after, out):
    out[...] = one[...] + other[...]


def add(one, other, after):
    return pl.pallas_call(
        add_kernel,
        out_shape=jax.ShapeDtypeStruct(one.shape, F32),
        in_specs=[VMEM, VMEM, pl.BlockSpec(memory_space=pl.ANY)],
        out_specs=VMEM,
        compiler_params=PARAMS,
        name="add",
    )(one, other, after)


def solve_kernel(target, last, places, *refs):
    whole, inverse_ref = refs[0], refs[1]
    count = 0 if last else target + 1
    factors = refs[2 : 2 + count]
    before = refs[2 + count : 2 + count + target]
    solved = refs[2 + count + target]
    held_inverse, held, sems = refs[-3:]
    fetch = pltpu.make_async_copy(inverse_ref.at[target], held_inverse, sems.at[0])
    fetch.start()
    copies = []
    for source in range(count):
        copy = pltpu.make_async_copy(factors[source].at[places[source]], held.at[source], sems.at[source + 1])
        copy.start()
        copies.append(copy)

    high, low = halves(whole[...].reshape(GROUP * SIDE, SIDE))
    right = jnp.concatenate([high, low], axis=1)
    fetch.wait()
    left, left_low = halves(held_inverse[...])
    wide = jnp.dot(left, right, preferred_element_type=F32)
    own = wide[:, :SIDE] + wide[:, SIDE:] + jnp.dot(left_low, high, preferred_element_type=F32)
    if last:
        for source in range(target):
            solved[source] = before[source][...]
        solved[target] = own
        return
    solved[...] = own
    terms = refs[-4]
    rights = [one[...] for one in before] + [own]
    for first in range(0, count, 2):
        some = range(first, min(first + 2, count))
        right = jnp.concatenate([rights[source] for source in some], axis=0)
        high, low = halves(right)
        right = jnp.concatenate([high, low], axis=1)
        for source in some:
            copies[source].wait()
        for part in range(4):
            rows = pl.ds(part * 4 * SIDE, 4 * SIDE)
            left = jnp.concatenate([held[source, rows] for source in some], axis=1)
            left, left_low = halves(left)
            wide = jnp.dot(left, right, preferred_element_type=F32)
            term = wide[:, :SIDE] + wide[:, SIDE:] + jnp.dot(left_low, high, preferred_element_type=F32)
            term = term.reshape(4, SIDE, SIDE)
            if first == 0:
                terms[pl.ds(part * 4, 4)] = term
            else:
                terms[pl.ds(part * 4, 4)] += term


def solve(target, whole, inverses, factors, before):
    last = target + 1 == inverses.shape[0]
    count = len(factors)
    one = jax.ShapeDtypeStruct((SIDE, SIDE), F32)
    out_shape = (one, jax.ShapeDtypeStruct((GROUP, SIDE, SIDE), F32))
    if last:
        out_shape = (jax.ShapeDtypeStruct((target + 1, SIDE, SIDE), F32),)
    hbm = pl.BlockSpec(memory_space=pltpu.HBM)
    out = pl.pallas_call(
        functools.partial(solve_kernel, target, last, tuple(block for _, block in factors)),
        out_shape=out_shape,
        in_specs=[VMEM, hbm] + [hbm] * count + [VMEM] * target,
        out_specs=(VMEM,) * len(out_shape),
        scratch_shapes=[
            pltpu.VMEM((SIDE, GROUP * SIDE), F32),
            pltpu.VMEM((max(count, 1), GROUP * SIDE, SIDE), F32),
            pltpu.SemaphoreType.DMA((count + 1,)),
        ],
        compiler_params=PARAMS,
        name="solve",
    )(whole, inverses, *[array for array, _ in factors], *before)
    return (out[0], None) if last else out


def hold_kernel(blocks, after, out):
    out[...] = blocks[1:]


def hold(blocks, after):
    shape = jax.ShapeDtypeStruct((blocks.shape[0] - 1,) + blocks.shape[1:], F32)
    return pl.pallas_call(
        hold_kernel,
        out_shape=shape,
        in_specs=[VMEM, pl.BlockSpec(memory_space=pl.ANY)],
        out_specs=VMEM,
        compiler_params=PARAMS,
        name="hold",
    )(blocks, after)


def to_group(parts):
    return lax.all_to_all(parts, COL, 0, 0)


def per_device(sire_index, dam_index, relatives, factor_blocks, inverses):
    old_dev, blocks, _ = relatives.shape
    here = jnp.stack([jnp.int32(0), jnp.int32(0), lax.axis_index("core"), lax.axis_index(ROW) * old_dev])
    here = here.astype(jnp.int32)
    swap = [(0, 1), (1, 0)]

    def gathered(some):
        return pltpu.with_memory_space_constraint(lax.all_gather(some, ROW, axis=1, tiled=True), pltpu.HBM)

    inverses = pltpu.with_memory_space_constraint(inverses, pltpu.HBM)
    first = first_block(factor_blocks)
    start = gathered(first)
    index = lax.all_to_all(pair_copies(sire_index[None], dam_index[None], first), ROW, 0, 0)

    def rows_of(first, count):
        rows = relatives[:, first : first + count, :].reshape(old_dev, count * SIDE).T
        return jnp.concatenate(pieces(rows))

    keep, give = select(1, here, index, rows_of(0, 1), here)
    first_terms = keep + lax.ppermute(give, "core", swap)
    relation0, copies = spread_first(lax.all_to_all(first_terms, "z", 0, 0))

    whole = to_group(copies)
    rest = gathered(hold(factor_blocks, relation0))

    keep, give = select(blocks - 1, here, index, rows_of(1, blocks - 1), first_terms)
    terms = add(keep, lax.ppermute(give, "core", swap), relation0)
    later = lax.psum_scatter(terms.reshape(-1, SIDE), "z", scatter_dimension=0, tiled=True)
    later = later.reshape(blocks - 1, SIDE, SIDE)

    solved = []
    for target in range(blocks):
        if target > 0:
            whole = to_group(spread(to_group(terms), later, target - 1))
        first = target * (target + 1) // 2
        factors = [(rest, first + source - 1) for source in range(target + 1)]
        if target == 0:
            factors = [(start, 0)]
        if target + 1 == blocks:
            factors = []
        own, terms = solve(target, whole, inverses, factors, solved)
        solved.append(own)
    relationship = jnp.concatenate([relation0[None], later])
    return relationship, solved[-1]


def solution(mesh):
    fine = Mesh(mesh.devices.reshape(8, 2, 4, 4), ROW + COL)
    return jax.shard_map(
        per_device,
        mesh=fine,
        in_specs=(
            P(ROW),
            P(ROW),
            P(ROW, None, COL),
            P(None, ROW, COL),
            P(None, COL, None),
        ),
        out_specs=(P(None, COL, ROW), P(None, COL, ROW)),
        check_vma=False,
    )
```

```python
import functools

import jax
import jax.numpy as jnp
from jax import lax
from jax.experimental import pallas as pl
from jax.experimental.pallas import tpu as pltpu
from jax.sharding import Mesh, PartitionSpec as P

ROW = ("z", "core")
COL = ("x", "y")
OLD = 512
SIDE = 128
GROUP = 16
LIMIT = 24 << 20
F32 = jnp.float32
BF16 = jnp.bfloat16
SMEM = pl.BlockSpec(memory_space=pltpu.SMEM)
VMEM = pl.BlockSpec(memory_space=pltpu.VMEM)
HBM = pl.BlockSpec(memory_space=pltpu.HBM)
PARAMS = pltpu.CompilerParams(vmem_limit_bytes=LIMIT)


def pieces(value):
    high = lax.reduce_precision(value, 8, 7)
    rest = value - high
    middle = lax.reduce_precision(rest, 8, 7)
    return [part.astype(BF16) for part in (high, middle, rest - middle)]


def halves(value):
    high = value.astype(BF16)
    return high, (value - high.astype(F32)).astype(BF16)


def select_kernel(count, here, index, rows, after, keep, give):
    core, base = here[2], here[3]
    ids = lax.broadcasted_iota(jnp.int32, (OLD, SIDE), 0) + base

    def picks(owner):
        pair = index[owner]
        sire = jnp.where(ids == pair[0:1, :], 0.5, 0.0)
        dam = jnp.where(ids == pair[1:2, :], 0.5, 0.0)
        return (sire + dam).astype(BF16)

    @pl.loop(0, 8)
    def _(z):
        both = jnp.concatenate([picks(2 * z + core), picks(2 * z + 1 - core)], axis=1)
        size = count * SIDE
        total = jnp.dot(rows[:size], both, preferred_element_type=F32)
        for piece in (1, 2):
            total += jnp.dot(rows[piece * size : (piece + 1) * size], both, preferred_element_type=F32)
        keep[z] = total[:, :SIDE]
        give[z] = total[:, SIDE:]


def select(count, here, index, rows, after):
    shape = jax.ShapeDtypeStruct((8, count * SIDE, SIDE), F32)
    return pl.pallas_call(
        functools.partial(select_kernel, count),
        out_shape=(shape, shape),
        in_specs=[SMEM, VMEM, VMEM, pl.BlockSpec(memory_space=pl.ANY)],
        out_specs=(VMEM, VMEM),
        cost_estimate=pl.CostEstimate(
            flops=2 * 3 * count * SIDE * OLD * 2048, bytes_accessed=count << 20, transcendentals=0
        ),
        compiler_params=PARAMS,
        name="select",
    )(here, index, rows, after)


def in_hbm(array):
    return pltpu.with_memory_space_constraint(array, pltpu.HBM)


def added(terms):
    total = terms[0]
    for part in range(1, terms.shape[0]):
        total += terms[part]
    return total


def first_kernel(terms, total_ref, copies):
    total = added(terms)
    total_ref[...] = total
    for owner in range(GROUP):
        copies[owner] = total


def spread_first(terms):
    return pl.pallas_call(
        first_kernel,
        out_shape=(
            jax.ShapeDtypeStruct((SIDE, SIDE), F32),
            jax.ShapeDtypeStruct((GROUP, SIDE, SIDE), F32),
        ),
        in_specs=[VMEM],
        out_specs=(VMEM, VMEM),
        compiler_params=PARAMS,
        name="sum_first",
    )(terms)


def subtract_kernel(block, terms, minuend, copies, held, sem):
    fetch = pltpu.make_async_copy(minuend.at[block], held, sem.at[0])
    fetch.start()
    total = added(terms)
    fetch.wait()
    total = held[...] - total
    for owner in range(GROUP):
        copies[owner] = total


def spread(terms, minuend, block):
    return pl.pallas_call(
        functools.partial(subtract_kernel, block),
        out_shape=jax.ShapeDtypeStruct((GROUP, SIDE, SIDE), F32),
        in_specs=[VMEM, HBM],
        out_specs=VMEM,
        scratch_shapes=[pltpu.VMEM((SIDE, SIDE), F32), pltpu.SemaphoreType.DMA((1,))],
        compiler_params=PARAMS,
        name="subtract",
    )(terms, in_hbm(minuend))


def first_block_kernel(blocks, out, sem):
    copy = pltpu.make_async_copy(blocks.at[0:1], out, sem.at[0])
    copy.start()
    copy.wait()


def first_block(blocks):
    return pl.pallas_call(
        first_block_kernel,
        out_shape=jax.ShapeDtypeStruct((1,) + blocks.shape[1:], F32),
        in_specs=[HBM],
        out_specs=VMEM,
        scratch_shapes=[pltpu.SemaphoreType.DMA((1,))],
        compiler_params=PARAMS,
        name="first_block",
    )(in_hbm(blocks))


def pair_kernel(sire, dam, after, pair, held, sems):
    copies = [
        pltpu.make_async_copy(sire, held.at[0:1], sems.at[0]),
        pltpu.make_async_copy(dam, held.at[1:2], sems.at[1]),
    ]
    for copy in copies:
        copy.start()
    for copy in copies:
        copy.wait()
    for owner in range(GROUP):
        pair[owner] = held[...]


def pair_copies(sire, dam, after):
    return pl.pallas_call(
        pair_kernel,
        out_shape=jax.ShapeDtypeStruct((GROUP, 2, SIDE), jnp.int32),
        in_specs=[HBM, HBM, pl.BlockSpec(memory_space=pl.ANY)],
        out_specs=VMEM,
        scratch_shapes=[pltpu.VMEM((2, SIDE), jnp.int32), pltpu.SemaphoreType.DMA((2,))],
        compiler_params=PARAMS,
        name="pair",
    )(in_hbm(sire), in_hbm(dam), after)


def solve_kernel(target, last, places, *refs):
    whole, inverse_ref = refs[0], refs[1]
    count = 0 if last else target + 1
    factors = refs[2 : 2 + count]
    before = refs[2 + count : 2 + count + target]
    solved = refs[2 + count + target]
    held_inverse, held, sems = refs[-3:]
    fetch = pltpu.make_async_copy(inverse_ref.at[target], held_inverse, sems.at[0])
    fetch.start()
    copies = []
    for source in range(count):
        copy = pltpu.make_async_copy(factors[source].at[places[source]], held.at[source], sems.at[source + 1])
        copy.start()
        copies.append(copy)

    high, low = halves(whole[...].reshape(GROUP * SIDE, SIDE))
    right = jnp.concatenate([high, low], axis=1)
    fetch.wait()
    left, left_low = halves(held_inverse[...])
    wide = jnp.dot(left, right, preferred_element_type=F32)
    own = wide[:, :SIDE] + wide[:, SIDE:] + jnp.dot(left_low, high, preferred_element_type=F32)
    if last:
        for source in range(target):
            solved[source] = before[source][...]
        solved[target] = own
        return
    solved[...] = own
    terms = refs[-4]
    rights = [one[...] for one in before] + [own]
    for first in range(0, count, 2):
        some = range(first, min(first + 2, count))
        right = jnp.concatenate([rights[source] for source in some], axis=0)
        high, low = halves(right)
        right = jnp.concatenate([high, low], axis=1)
        for source in some:
            copies[source].wait()
        for part in range(4):
            rows = pl.ds(part * 4 * SIDE, 4 * SIDE)
            left = jnp.concatenate([held[source, rows] for source in some], axis=1)
            left, left_low = halves(left)
            wide = jnp.dot(left, right, preferred_element_type=F32)
            term = wide[:, :SIDE] + wide[:, SIDE:] + jnp.dot(left_low, high, preferred_element_type=F32)
            term = term.reshape(4, SIDE, SIDE)
            if first == 0:
                terms[pl.ds(part * 4, 4)] = term
            else:
                terms[pl.ds(part * 4, 4)] += term


def solve(target, whole, inverses, factors, before):
    last = target + 1 == inverses.shape[0]
    count = len(factors)
    one = jax.ShapeDtypeStruct((SIDE, SIDE), F32)
    out_shape = (one, jax.ShapeDtypeStruct((GROUP, SIDE, SIDE), F32))
    if last:
        out_shape = (jax.ShapeDtypeStruct((target + 1, SIDE, SIDE), F32),)
    hbm = pl.BlockSpec(memory_space=pltpu.HBM)
    out = pl.pallas_call(
        functools.partial(solve_kernel, target, last, tuple(block for _, block in factors)),
        out_shape=out_shape,
        in_specs=[VMEM, hbm] + [hbm] * count + [VMEM] * target,
        out_specs=(VMEM,) * len(out_shape),
        scratch_shapes=[
            pltpu.VMEM((SIDE, GROUP * SIDE), F32),
            pltpu.VMEM((max(count, 1), GROUP * SIDE, SIDE), F32),
            pltpu.SemaphoreType.DMA((count + 1,)),
        ],
        compiler_params=PARAMS,
        name="solve",
    )(whole, inverses, *[array for array, _ in factors], *before)
    return (out[0], None) if last else out


def hold_kernel(blocks, after, out):
    out[...] = blocks[1:]


def hold(blocks, after):
    shape = jax.ShapeDtypeStruct((blocks.shape[0] - 1,) + blocks.shape[1:], F32)
    return pl.pallas_call(
        hold_kernel,
        out_shape=shape,
        in_specs=[VMEM, pl.BlockSpec(memory_space=pl.ANY)],
        out_specs=VMEM,
        compiler_params=PARAMS,
        name="hold",
    )(blocks, after)


def to_group(parts):
    return lax.all_to_all(parts, COL, 0, 0)


def per_device(sire_index, dam_index, relatives, factor_blocks, inverses):
    old_dev, blocks, _ = relatives.shape
    here = jnp.stack([jnp.int32(0), jnp.int32(0), lax.axis_index("core"), lax.axis_index(ROW) * old_dev])
    here = here.astype(jnp.int32)
    swap = [(0, 1), (1, 0)]

    def gathered(some):
        return pltpu.with_memory_space_constraint(lax.all_gather(some, ROW, axis=1, tiled=True), pltpu.HBM)

    inverses = pltpu.with_memory_space_constraint(inverses, pltpu.HBM)
    first = first_block(factor_blocks)
    start = gathered(first)
    index = lax.all_to_all(pair_copies(sire_index[None], dam_index[None], first), ROW, 0, 0)

    def rows_of(first, count):
        rows = relatives[:, first : first + count, :].reshape(old_dev, count * SIDE).T
        return jnp.concatenate(pieces(rows))

    keep, give = select(1, here, index, rows_of(0, 1), here)
    first_terms = keep + lax.ppermute(give, "core", swap)
    relation0, copies = spread_first(lax.all_to_all(first_terms, "z", 0, 0))

    whole = to_group(copies)
    rest = gathered(hold(factor_blocks, relation0))

    keep, give = select(blocks - 1, here, index, rows_of(1, blocks - 1), first_terms)
    terms = keep + lax.ppermute(give, "core", swap)
    later = lax.psum_scatter(terms.reshape(-1, SIDE), "z", scatter_dimension=0, tiled=True)
    later = later.reshape(blocks - 1, SIDE, SIDE)

    solved = []
    for target in range(blocks):
        if target > 0:
            whole = to_group(spread(to_group(terms), later, target - 1))
        first = target * (target + 1) // 2
        factors = [(rest, first + source - 1) for source in range(target + 1)]
        if target == 0:
            factors = [(start, 0)]
        if target + 1 == blocks:
            factors = []
        own, terms = solve(target, whole, inverses, factors, solved)
        solved.append(own)
    relationship = jnp.concatenate([relation0[None], later])
    return relationship, solved[-1]


def solution(mesh):
    fine = Mesh(mesh.devices.reshape(8, 2, 4, 4), ROW + COL)
    return jax.shard_map(
        per_device,
        mesh=fine,
        in_specs=(
            P(ROW),
            P(ROW),
            P(ROW, None, COL),
            P(None, ROW, COL),
            P(None, COL, None),
        ),
        out_specs=(P(None, COL, ROW), P(None, COL, ROW)),
        check_vma=False,
    )
```

```python
import functools

import jax
import jax.numpy as jnp
from jax import lax
from jax.experimental import pallas as pl
from jax.experimental.pallas import tpu as pltpu
from jax.sharding import Mesh, PartitionSpec as P

ROW = ("z", "core")
COL = ("x", "y")
OLD = 512
SIDE = 128
GROUP = 16
LIMIT = 24 << 20
F32 = jnp.float32
BF16 = jnp.bfloat16
SMEM = pl.BlockSpec(memory_space=pltpu.SMEM)
VMEM = pl.BlockSpec(memory_space=pltpu.VMEM)
PARAMS = pltpu.CompilerParams(vmem_limit_bytes=LIMIT)


def pieces(value):
    high = lax.reduce_precision(value, 8, 7)
    rest = value - high
    middle = lax.reduce_precision(rest, 8, 7)
    return [part.astype(BF16) for part in (high, middle, rest - middle)]


def halves(value):
    high = value.astype(BF16)
    return high, (value - high.astype(F32)).astype(BF16)


def select_kernel(count, here, index, rows, after, keep, give):
    core, base = here[2], here[3]
    ids = lax.broadcasted_iota(jnp.int32, (OLD, SIDE), 0) + base

    def picks(owner):
        pair = index[owner]
        sire = jnp.where(ids == pair[0:1, :], 0.5, 0.0)
        dam = jnp.where(ids == pair[1:2, :], 0.5, 0.0)
        return (sire + dam).astype(BF16)

    @pl.loop(0, 8)
    def _(z):
        both = jnp.concatenate([picks(2 * z + core), picks(2 * z + 1 - core)], axis=1)
        size = count * SIDE
        total = jnp.dot(rows[:size], both, preferred_element_type=F32)
        for piece in (1, 2):
            total += jnp.dot(rows[piece * size : (piece + 1) * size], both, preferred_element_type=F32)
        keep[z] = total[:, :SIDE]
        give[z] = total[:, SIDE:]


def select(count, here, index, rows, after):
    shape = jax.ShapeDtypeStruct((8, count * SIDE, SIDE), F32)
    return pl.pallas_call(
        functools.partial(select_kernel, count),
        out_shape=(shape, shape),
        in_specs=[SMEM, VMEM, VMEM, pl.BlockSpec(memory_space=pl.ANY)],
        out_specs=(VMEM, VMEM),
        cost_estimate=pl.CostEstimate(
            flops=2 * 3 * count * SIDE * OLD * 2048, bytes_accessed=count << 20, transcendentals=0
        ),
        compiler_params=PARAMS,
        name="select",
    )(here, index, rows, after)


def remain_kernel(block, *refs):
    terms = refs[0]
    if block is not None:
        held, sem = refs[3:]
        fetch = pltpu.make_async_copy(refs[1].at[block], held, sem.at[0])
        fetch.start()
    total = terms[0]
    for part in range(1, terms.shape[0]):
        total += terms[part]
    if block is None:
        refs[1][...] = total
    else:
        fetch.wait()
        total = held[...] - total
    for owner in range(GROUP):
        refs[2][owner] = total


def spread(terms, minuend=None, block=None):
    copies = jax.ShapeDtypeStruct((GROUP, SIDE, SIDE), F32)
    if minuend is None:
        return pl.pallas_call(
            functools.partial(remain_kernel, None),
            out_shape=(jax.ShapeDtypeStruct((SIDE, SIDE), F32), copies),
            in_specs=[VMEM],
            out_specs=(VMEM, VMEM),
            compiler_params=PARAMS,
            name="sum_first",
        )(terms)
    return pl.pallas_call(
        functools.partial(remain_kernel, block),
        out_shape=copies,
        in_specs=[VMEM, pl.BlockSpec(memory_space=pltpu.HBM)],
        out_specs=VMEM,
        scratch_shapes=[pltpu.VMEM((SIDE, SIDE), F32), pltpu.SemaphoreType.DMA((1,))],
        compiler_params=PARAMS,
        name="subtract",
    )(terms, pltpu.with_memory_space_constraint(minuend, pltpu.HBM))


def solve_kernel(target, last, places, *refs):
    whole, inverse_ref = refs[0], refs[1]
    count = 0 if last else target + 1
    factors = refs[2 : 2 + count]
    before = refs[2 + count : 2 + count + target]
    solved = refs[2 + count + target]
    held_inverse, held, sems = refs[-3:]
    fetch = pltpu.make_async_copy(inverse_ref.at[target], held_inverse, sems.at[0])
    fetch.start()
    copies = []
    for source in range(count):
        copy = pltpu.make_async_copy(factors[source].at[places[source]], held.at[source], sems.at[source + 1])
        copy.start()
        copies.append(copy)

    high, low = halves(whole[...].reshape(GROUP * SIDE, SIDE))
    right = jnp.concatenate([high, low], axis=1)
    fetch.wait()
    left, left_low = halves(held_inverse[...])
    wide = jnp.dot(left, right, preferred_element_type=F32)
    own = wide[:, :SIDE] + wide[:, SIDE:] + jnp.dot(left_low, high, preferred_element_type=F32)
    if last:
        for source in range(target):
            solved[source] = before[source][...]
        solved[target] = own
        return
    solved[...] = own
    terms = refs[-4]
    rights = [one[...] for one in before] + [own]
    for first in range(0, count, 2):
        some = range(first, min(first + 2, count))
        right = jnp.concatenate([rights[source] for source in some], axis=0)
        high, low = halves(right)
        right = jnp.concatenate([high, low], axis=1)
        for source in some:
            copies[source].wait()
        for part in range(4):
            rows = pl.ds(part * 4 * SIDE, 4 * SIDE)
            left = jnp.concatenate([held[source, rows] for source in some], axis=1)
            left, left_low = halves(left)
            wide = jnp.dot(left, right, preferred_element_type=F32)
            term = wide[:, :SIDE] + wide[:, SIDE:] + jnp.dot(left_low, high, preferred_element_type=F32)
            term = term.reshape(4, SIDE, SIDE)
            if first == 0:
                terms[pl.ds(part * 4, 4)] = term
            else:
                terms[pl.ds(part * 4, 4)] += term


def solve(target, whole, inverses, factors, before):
    last = target + 1 == inverses.shape[0]
    count = len(factors)
    one = jax.ShapeDtypeStruct((SIDE, SIDE), F32)
    out_shape = (one, jax.ShapeDtypeStruct((GROUP, SIDE, SIDE), F32))
    if last:
        out_shape = (jax.ShapeDtypeStruct((target + 1, SIDE, SIDE), F32),)
    hbm = pl.BlockSpec(memory_space=pltpu.HBM)
    out = pl.pallas_call(
        functools.partial(solve_kernel, target, last, tuple(block for _, block in factors)),
        out_shape=out_shape,
        in_specs=[VMEM, hbm] + [hbm] * count + [VMEM] * target,
        out_specs=(VMEM,) * len(out_shape),
        scratch_shapes=[
            pltpu.VMEM((SIDE, GROUP * SIDE), F32),
            pltpu.VMEM((max(count, 1), GROUP * SIDE, SIDE), F32),
            pltpu.SemaphoreType.DMA((count + 1,)),
        ],
        compiler_params=PARAMS,
        name="solve",
    )(whole, inverses, *[array for array, _ in factors], *before)
    return (out[0], None) if last else out


def hold_kernel(blocks, after, out):
    out[...] = blocks[1:]


def hold(blocks, after):
    shape = jax.ShapeDtypeStruct((blocks.shape[0] - 1,) + blocks.shape[1:], F32)
    return pl.pallas_call(
        hold_kernel,
        out_shape=shape,
        in_specs=[VMEM, pl.BlockSpec(memory_space=pl.ANY)],
        out_specs=VMEM,
        compiler_params=PARAMS,
        name="hold",
    )(blocks, after)


def to_group(parts):
    return lax.all_to_all(parts, COL, 0, 0)


def per_device(sire_index, dam_index, relatives, factor_blocks, inverses):
    old_dev, blocks, _ = relatives.shape
    here = jnp.stack([jnp.int32(0), jnp.int32(0), lax.axis_index("core"), lax.axis_index(ROW) * old_dev])
    here = here.astype(jnp.int32)
    swap = [(0, 1), (1, 0)]

    def gathered(some):
        return pltpu.with_memory_space_constraint(lax.all_gather(some, ROW, axis=1, tiled=True), pltpu.HBM)

    start = gathered(factor_blocks[:1])
    inverses = pltpu.with_memory_space_constraint(inverses, pltpu.HBM)

    pair = jnp.stack([sire_index, dam_index])
    index = lax.all_to_all(jnp.broadcast_to(pair[None], (GROUP, 2, SIDE)), ROW, 0, 0)

    def rows_of(first, count):
        rows = relatives[:, first : first + count, :].reshape(old_dev, count * SIDE).T
        return jnp.concatenate(pieces(rows))

    keep, give = select(1, here, index, rows_of(0, 1), here)
    first_terms = keep + lax.ppermute(give, "core", swap)
    relation0, copies = spread(lax.all_to_all(first_terms, "z", 0, 0))

    rest = gathered(hold(factor_blocks, relation0))

    keep, give = select(blocks - 1, here, index, rows_of(1, blocks - 1), first_terms)
    terms = keep + lax.ppermute(give, "core", swap)
    later = lax.psum_scatter(terms.reshape(-1, SIDE), "z", scatter_dimension=0, tiled=True)
    later = later.reshape(blocks - 1, SIDE, SIDE)

    solved = []
    for target in range(blocks):
        if target > 0:
            copies = spread(to_group(terms), later, target - 1)
        first = target * (target + 1) // 2
        factors = [(rest, first + source - 1) for source in range(target + 1)]
        if target == 0:
            factors = [(start, 0)]
        if target + 1 == blocks:
            factors = []
        own, terms = solve(target, to_group(copies), inverses, factors, solved)
        solved.append(own)
    relationship = jnp.concatenate([relation0[None], later])
    return relationship, solved[-1]


def solution(mesh):
    fine = Mesh(mesh.devices.reshape(8, 2, 4, 4), ROW + COL)
    return jax.shard_map(
        per_device,
        mesh=fine,
        in_specs=(
            P(ROW),
            P(ROW),
            P(ROW, None, COL),
            P(None, ROW, COL),
            P(None, COL, None),
        ),
        out_specs=(P(None, COL, ROW), P(None, COL, ROW)),
        check_vma=False,
    )
```

```python
import functools

import jax
import jax.numpy as jnp
from jax import lax
from jax.experimental import pallas as pl
from jax.experimental.pallas import tpu as pltpu
from jax.sharding import Mesh, PartitionSpec as P

ROW = ("z", "core")
COL = ("x", "y")
OLD = 512
SIDE = 128
GROUP = 16
LIMIT = 24 << 20
F32 = jnp.float32
BF16 = jnp.bfloat16
SMEM = pl.BlockSpec(memory_space=pltpu.SMEM)
VMEM = pl.BlockSpec(memory_space=pltpu.VMEM)
PARAMS = pltpu.CompilerParams(vmem_limit_bytes=LIMIT)


def pieces(value):
    high = lax.reduce_precision(value, 8, 7)
    rest = value - high
    middle = lax.reduce_precision(rest, 8, 7)
    return [part.astype(BF16) for part in (high, middle, rest - middle)]


def halves(value):
    high = value.astype(BF16)
    return high, (value - high.astype(F32)).astype(BF16)


def select_kernel(count, here, index, rows, after, keep, give):
    core, base = here[2], here[3]
    ids = lax.broadcasted_iota(jnp.int32, (OLD, SIDE), 0) + base

    def picks(owner):
        pair = index[owner]
        sire = jnp.where(ids == pair[0:1, :], 0.5, 0.0)
        dam = jnp.where(ids == pair[1:2, :], 0.5, 0.0)
        return (sire + dam).astype(BF16)

    @pl.loop(0, 8)
    def _(z):
        both = jnp.concatenate([picks(2 * z + core), picks(2 * z + 1 - core)], axis=1)
        size = count * SIDE
        total = jnp.dot(rows[:size], both, preferred_element_type=F32)
        for piece in (1, 2):
            total += jnp.dot(rows[piece * size : (piece + 1) * size], both, preferred_element_type=F32)
        keep[z] = total[:, :SIDE]
        give[z] = total[:, SIDE:]


def select(count, here, index, rows, after):
    shape = jax.ShapeDtypeStruct((8, count * SIDE, SIDE), F32)
    return pl.pallas_call(
        functools.partial(select_kernel, count),
        out_shape=(shape, shape),
        in_specs=[SMEM, VMEM, VMEM, pl.BlockSpec(memory_space=pl.ANY)],
        out_specs=(VMEM, VMEM),
        cost_estimate=pl.CostEstimate(
            flops=2 * 3 * count * SIDE * OLD * 2048, bytes_accessed=count << 20, transcendentals=0
        ),
        compiler_params=PARAMS,
        name="select",
    )(here, index, rows, after)


def remain_kernel(block, *refs):
    terms = refs[0]
    total = terms[0]
    for part in range(1, terms.shape[0]):
        total += terms[part]
    if block is None:
        refs[1][...] = total
    else:
        total = refs[1][block] - total
    for owner in range(GROUP):
        refs[2][owner] = total


def spread(terms, minuend=None, block=None):
    copies = jax.ShapeDtypeStruct((GROUP, SIDE, SIDE), F32)
    if minuend is None:
        return pl.pallas_call(
            functools.partial(remain_kernel, None),
            out_shape=(jax.ShapeDtypeStruct((SIDE, SIDE), F32), copies),
            in_specs=[VMEM],
            out_specs=(VMEM, VMEM),
            compiler_params=PARAMS,
            name="sum_first",
        )(terms)
    return pl.pallas_call(
        functools.partial(remain_kernel, block),
        out_shape=copies,
        in_specs=[VMEM, VMEM],
        out_specs=VMEM,
        compiler_params=PARAMS,
        name="subtract",
    )(terms, minuend)


def solve_kernel(target, last, places, *refs):
    whole, inverse_ref = refs[0], refs[1]
    count = 0 if last else target + 1
    factors = refs[2 : 2 + count]
    before = refs[2 + count : 2 + count + target]
    extra = 2 if last else 0
    solved = refs[2 + count + target + extra]
    held_inverse, held, sems = refs[-3:]
    fetch = pltpu.make_async_copy(inverse_ref.at[target], held_inverse, sems.at[0])
    fetch.start()
    copies = []
    for source in range(count):
        copy = pltpu.make_async_copy(factors[source].at[places[source]], held.at[source], sems.at[source + 1])
        copy.start()
        copies.append(copy)

    high, low = halves(whole[...].reshape(GROUP * SIDE, SIDE))
    right = jnp.concatenate([high, low], axis=1)
    fetch.wait()
    left, left_low = halves(held_inverse[...])
    wide = jnp.dot(left, right, preferred_element_type=F32)
    own = wide[:, :SIDE] + wide[:, SIDE:] + jnp.dot(left_low, high, preferred_element_type=F32)
    if last:
        for source in range(target):
            solved[source] = before[source][...]
        solved[target] = own
        refs[-4][0] = refs[2 + target][...]
        refs[-4][1:] = refs[3 + target][...]
        return
    solved[...] = own
    terms = refs[-4]
    rights = [one[...] for one in before] + [own]
    for first in range(0, count, 2):
        some = range(first, min(first + 2, count))
        right = jnp.concatenate([rights[source] for source in some], axis=0)
        high, low = halves(right)
        right = jnp.concatenate([high, low], axis=1)
        for source in some:
            copies[source].wait()
        for part in range(4):
            rows = pl.ds(part * 4 * SIDE, 4 * SIDE)
            left = jnp.concatenate([held[source, rows] for source in some], axis=1)
            left, left_low = halves(left)
            wide = jnp.dot(left, right, preferred_element_type=F32)
            term = wide[:, :SIDE] + wide[:, SIDE:] + jnp.dot(left_low, high, preferred_element_type=F32)
            term = term.reshape(4, SIDE, SIDE)
            if first == 0:
                terms[pl.ds(part * 4, 4)] = term
            else:
                terms[pl.ds(part * 4, 4)] += term


def solve(target, whole, inverses, factors, before, relation):
    last = target + 1 == inverses.shape[0]
    count = len(factors)
    one = jax.ShapeDtypeStruct((SIDE, SIDE), F32)
    out_shape = (one, jax.ShapeDtypeStruct((GROUP, SIDE, SIDE), F32))
    if last:
        before = [*before, *relation]
        out_shape = (jax.ShapeDtypeStruct((target + 1, SIDE, SIDE), F32),) * 2
    hbm = pl.BlockSpec(memory_space=pltpu.HBM)
    out = pl.pallas_call(
        functools.partial(solve_kernel, target, last, tuple(block for _, block in factors)),
        out_shape=out_shape,
        in_specs=[VMEM, hbm] + [hbm] * count + [VMEM] * len(before),
        out_specs=(VMEM,) * len(out_shape),
        scratch_shapes=[
            pltpu.VMEM((SIDE, GROUP * SIDE), F32),
            pltpu.VMEM((max(count, 1), GROUP * SIDE, SIDE), F32),
            pltpu.SemaphoreType.DMA((count + 1,)),
        ],
        compiler_params=PARAMS,
        name="solve",
    )(whole, inverses, *[array for array, _ in factors], *before)
    return out


def hold_kernel(blocks, after, out):
    out[...] = blocks[1:]


def hold(blocks, after):
    shape = jax.ShapeDtypeStruct((blocks.shape[0] - 1,) + blocks.shape[1:], F32)
    return pl.pallas_call(
        hold_kernel,
        out_shape=shape,
        in_specs=[VMEM, pl.BlockSpec(memory_space=pl.ANY)],
        out_specs=VMEM,
        compiler_params=PARAMS,
        name="hold",
    )(blocks, after)


def to_group(parts):
    return lax.all_to_all(parts, COL, 0, 0)


def per_device(sire_index, dam_index, relatives, factor_blocks, inverses):
    old_dev, blocks, _ = relatives.shape
    here = jnp.stack([jnp.int32(0), jnp.int32(0), lax.axis_index("core"), lax.axis_index(ROW) * old_dev])
    here = here.astype(jnp.int32)
    swap = [(0, 1), (1, 0)]

    def gathered(some):
        return pltpu.with_memory_space_constraint(lax.all_gather(some, ROW, axis=1, tiled=True), pltpu.HBM)

    start = gathered(factor_blocks[:1])
    inverses = pltpu.with_memory_space_constraint(inverses, pltpu.HBM)

    pair = jnp.stack([sire_index, dam_index])
    index = lax.all_to_all(jnp.broadcast_to(pair[None], (GROUP, 2, SIDE)), ROW, 0, 0)

    def rows_of(first, count):
        rows = relatives[:, first : first + count, :].reshape(old_dev, count * SIDE).T
        return jnp.concatenate(pieces(rows))

    keep, give = select(1, here, index, rows_of(0, 1), here)
    first_terms = keep + lax.ppermute(give, "core", swap)
    relation0, copies = spread(lax.all_to_all(first_terms, "z", 0, 0))

    rest = gathered(hold(factor_blocks, relation0))

    keep, give = select(blocks - 1, here, index, rows_of(1, blocks - 1), first_terms)
    terms = keep + lax.ppermute(give, "core", swap)
    later = lax.psum_scatter(terms.reshape(-1, SIDE), "z", scatter_dimension=0, tiled=True)
    later = later.reshape(blocks - 1, SIDE, SIDE)

    solved = []
    for target in range(blocks):
        if target > 0:
            copies = spread(to_group(terms), later, target - 1)
        first = target * (target + 1) // 2
        factors = [(rest, first + source - 1) for source in range(target + 1)]
        if target == 0:
            factors = [(start, 0)]
        if target + 1 == blocks:
            factors = []
        own, terms = solve(target, to_group(copies), inverses, factors, solved, (relation0, later))
        solved.append(own)
    return terms, solved[-1]


def solution(mesh):
    fine = Mesh(mesh.devices.reshape(8, 2, 4, 4), ROW + COL)
    return jax.shard_map(
        per_device,
        mesh=fine,
        in_specs=(
            P(ROW),
            P(ROW),
            P(ROW, None, COL),
            P(None, ROW, COL),
            P(None, COL, None),
        ),
        out_specs=(P(None, COL, ROW), P(None, COL, ROW)),
        check_vma=False,
    )
```
